512 devices in a mesh: member: 16 (over y, x_lo, core), patch: 32 (over z, x_hi).
Axes of the slice: x: 4 (x_hi: 2, x_lo: 2; x = x_hi * 2 + x_lo), y: 4, z: 16, core: 2. Of those that a mesh axis runs over, the one named last changes fastest.
Arguments:
- kernel_rows: bfloat16 [8192, 8192], P('patch'), as said below
- row_scale: float32 [8192], P('patch'), may hold values from 0.3 to 1
- self_stiffness: float32 [8192], P('patch'), may hold values from 1 to 3
- base_stress: float32 [8192], P('patch'), may hold values from 0.5 to 2.5
- friction_rate: float32 [8192], P('patch'), may hold values from 0.5 to 2
- damping: float32 [8192], P('patch'), may hold values from 0.5 to 2
- deficit_start: float32 [96, 8192], P('member', 'patch'), may hold values from -3 to 3
- state_start: float32 [96, 8192], P('member', 'patch'), may hold values from -1 to 1
- obs_rate: float32 [8192], P('patch'), may hold values from -6 to 6
- obs_precision: float32 [8192], P('patch'), may hold values from 0.2 to 2
Outputs:
- analysis: float32 [3, 96, 32, 256], P(None, None, 'patch', 'member')
The draws below stay inside these ranges and needn't reach their ends.
Inputs may be any that keep to these rules, and one draw needn't show every extreme that they name: `kernel_rows`: entries are independent with mean zero and root mean square of order 8192 ** -0.5 times a per-row factor.
All inputs are finite; a program needn't handle non-finite values.
Results may differ from the reference program's by a relative error of at most 0.0006.
Values may be sent and summed in bfloat16 or wider, within the bound.
No kernel may reach another device: no remote copies, remote signals or barrier semaphores. Data moves between devices by JAX's collectives and lax.ppermute only.
A program may use at most 64 MiB of HBM per device.

```python
import math
import jax
import jax.numpy as jnp
from jax import lax

PATCH_DEV = 256
STEPS = 2
NEWTON = 4
NS_ITERS = 6
MARGIN = 8
PATCHES = 8192
ENSEMBLE = 96
BLOCK = 16
N_PATCH = 32


def draw_kernel_rows(key, part):
    entry_key = jax.random.fold_in(key, 11)
    spread = PATCHES ** (-0.5)
    values = jax.random.normal(entry_key, (PATCHES, PATCHES), jnp.float32) * spread
    return values.astype(jnp.bfloat16)


def block_scale(key, shape, pieces, least, top_value):
    def one(position, parts):
        steps = jax.random.uniform(jax.random.fold_in(jax.random.fold_in(key, 6), position), (parts,), jnp.float32, least / len(pieces), top_value / len(pieces))
        return jnp.repeat(jnp.exp(steps), shape[position] // parts).reshape((-1,) + (1,) * (len(shape) - position - 1))

    loudness = one(*pieces[0])
    for cut in pieces[1:]:
        loudness = loudness * one(*cut)
    return loudness


def gaussian(own_key, extent, width, limit, shards=(), kind=jnp.bfloat16):
    loudness = block_scale(own_key, extent, shards, -0.22, 0.18) if shards else 1.0
    array = jax.random.normal(own_key, extent, jnp.float32) * width * loudness
    return jnp.minimum(jnp.maximum(array, -limit), limit).astype(kind)


def setup_inputs(seed: int = 0) -> dict:
    key_of = jax.random.split(jax.random.key(seed), 11)
    return {
        "kernel_rows": draw_kernel_rows(jax.random.fold_in(key_of[10], 71), 0),
        "row_scale": jnp.clip(jnp.exp(math.log(1.0) - 1.2039728 * jax.random.uniform(key_of[1], (PATCHES,), jnp.float32) ** block_scale(key_of[1], (PATCHES,), ((0, 32),), -0.2, 0.2)), 0.3, 1.0),
        "self_stiffness": jnp.clip(jnp.exp(math.log(3.0) - 1.0986123 * jax.random.uniform(key_of[2], (PATCHES,), jnp.float32) ** block_scale(key_of[2], (PATCHES,), ((0, 32),), -0.2, 0.2)), 1.0, 3.0),
        "base_stress": jnp.clip(0.5 + 2.0 * jax.random.uniform(key_of[3], (PATCHES,), jnp.float32) ** block_scale(key_of[3], (PATCHES,), ((0, 32),), -0.2, 0.2), 0.5, 2.5),
        "friction_rate": jnp.clip(jnp.exp(math.log(2.0) - 1.3862944 * jax.random.uniform(key_of[4], (PATCHES,), jnp.float32) ** block_scale(key_of[4], (PATCHES,), ((0, 32),), -0.2, 0.2)), 0.5, 2.0),
        "damping": jnp.clip(jnp.exp(math.log(2.0) - 1.3862944 * jax.random.uniform(key_of[5], (PATCHES,), jnp.float32) ** block_scale(key_of[5], (PATCHES,), ((0, 32),), -0.2, 0.2)), 0.5, 2.0),
        "deficit_start": gaussian(key_of[6], (ENSEMBLE, PATCHES), 0.5, 3.0, ((0, 16), (1, 32)), jnp.float32),
        "state_start": jnp.clip(jax.random.uniform(key_of[7], (ENSEMBLE, PATCHES), jnp.float32, -1.0, 1.0) * block_scale(key_of[7], (ENSEMBLE, PATCHES), ((0, 16), (1, 32)), -0.4, 0.0), -1.0, 1.0),
        "obs_rate": gaussian(key_of[8], (PATCHES,), 1.0, 6.0, ((0, 32),), jnp.float32),
        "obs_precision": jnp.clip(jnp.exp(math.log(2.0) - 2.3025851 * jax.random.uniform(key_of[9], (PATCHES,), jnp.float32) ** block_scale(key_of[9], (PATCHES,), ((0, 32),), -0.2, 0.2)), 0.2, 2.0),
    }


time_step = 0.25
plate_rate = 1.0

def inverse_sinh(value):
    magnitude = jnp.abs(value)
    result = jnp.log(magnitude + jnp.sqrt(magnitude * magnitude + 1.0))
    return jnp.where(value < 0, -result, result)

def slip_rate(stress, state_log, guess, friction_rate, damping):
    factor = 0.5 * jnp.exp(state_log / friction_rate)
    velocity = guess
    for _ in range(NEWTON):
        scaled = factor * velocity
        residual = friction_rate * inverse_sinh(scaled) + damping * velocity - stress
        derivative = friction_rate * factor / jnp.sqrt(1.0 + scaled * scaled) + damping
        velocity = velocity - residual / derivative
    return velocity

def analyse(local_state, rate_window, obs_window):
    ensemble = rate_window.shape[0]
    window_width = rate_window.shape[1]
    sub_block = local_state.shape[2]
    margin = (window_width - sub_block) // 2
    highest = lax.Precision.HIGHEST
    mean_rate = lax.optimization_barrier(jnp.mean(rate_window, axis=0))
    anomalies = rate_window - mean_rate[None, :]
    innovation = obs_window[0] - mean_rate
    distance = jnp.abs(jnp.arange(sub_block, dtype=jnp.int32)[:, None] + margin - jnp.arange(window_width, dtype=jnp.int32)[None, :]).astype(jnp.float32)
    tapering = jnp.where(distance <= margin, jnp.exp(-0.5 * (distance / margin) ** 2), 0.0)
    weights = tapering * obs_window[1][None, :]
    weighted = anomalies[None, :, :] * weights[:, None, :]
    cross_terms = jnp.einsum('imj,nj->imn', weighted, anomalies, precision=highest)
    drive_terms = jnp.einsum('imj,j->im', weighted, innovation, precision=highest)
    identity = jnp.eye(ensemble, dtype=jnp.float32)
    scaling = ensemble - 1.0 + jnp.trace(cross_terms, axis1=1, axis2=2)
    root_part = ((ensemble - 1.0) * identity[None] + cross_terms) / scaling[:, None, None]
    inverse_root = jnp.broadcast_to(identity, root_part.shape)
    for _ in range(NS_ITERS):
        mixing = 1.5 * identity[None] - 0.5 * jnp.matmul(inverse_root, root_part, precision=highest)
        root_part = jnp.matmul(root_part, mixing, precision=highest)
        inverse_root = jnp.matmul(mixing, inverse_root, precision=highest)
    half_step = jnp.einsum('imn,in->im', inverse_root, drive_terms, precision=highest)
    mean_weight = jnp.einsum('imn,in->im', inverse_root, half_step, precision=highest) / scaling[:, None]
    spread = jnp.sqrt(ensemble - 1.0) * inverse_root / jnp.sqrt(scaling)[:, None, None]
    combined = spread + mean_weight[:, :, None]
    state_mean = lax.optimization_barrier(jnp.mean(local_state, axis=1))
    state_spread = local_state - state_mean[:, None, :]
    return state_mean[:, None, :] + jnp.einsum('vmi,imk->vki', state_spread, combined, precision=highest)

def reference(kernel_rows, row_scale, self_stiffness, base_stress, friction_rate, damping, deficit_start, state_start, obs_rate, obs_precision):
    kernel_wide = kernel_rows.astype(jnp.float32)

    def stress_of(deficit):
        rounded = lax.optimization_barrier(deficit.astype(jnp.bfloat16))
        coupled = jnp.dot(rounded.astype(jnp.float32), kernel_wide.T, precision=lax.Precision.HIGHEST)
        return base_stress + self_stiffness * deficit + row_scale * coupled

    def tendency(deficit, state_log, guess):
        velocity = slip_rate(stress_of(deficit), state_log, guess, friction_rate, damping)
        return (plate_rate - velocity, jnp.exp(-state_log) - jnp.abs(velocity), velocity)
    deficit = deficit_start
    state_log = state_start
    velocity = jnp.zeros_like(deficit_start)
    for _ in range(STEPS):
        deficit_zero, state_zero = (deficit, state_log)
        change, state_change, velocity = tendency(deficit_zero, state_zero, velocity)
        deficit_one = deficit_zero + time_step * change
        state_one = state_zero + time_step * state_change
        change, state_change, velocity = tendency(deficit_one, state_one, velocity)
        deficit_two = 0.75 * deficit_zero + 0.25 * (deficit_one + time_step * change)
        state_two = 0.75 * state_zero + 0.25 * (state_one + time_step * state_change)
        change, state_change, velocity = tendency(deficit_two, state_two, velocity)
        deficit = deficit_zero / 3.0 + 2.0 / 3.0 * (deficit_two + time_step * change)
        state_log = state_zero / 3.0 + 2.0 / 3.0 * (state_two + time_step * state_change)
    velocity = slip_rate(stress_of(deficit), state_log, velocity, friction_rate, damping)
    stacked = jnp.stack([deficit, state_log, velocity])
    ensemble = deficit.shape[0]
    blocks_total = PATCHES // BLOCK
    window_width = BLOCK + 2 * MARGIN
    positions = jnp.arange(blocks_total, dtype=jnp.int32)[:, None] * BLOCK + jnp.arange(window_width, dtype=jnp.int32)[None, :]
    padded_rate = jnp.pad(velocity, ((0, 0), (MARGIN, MARGIN)))
    padded_obs = jnp.pad(jnp.stack([obs_rate, obs_precision]), ((0, 0), (MARGIN, MARGIN)))
    rate_windows = jnp.transpose(padded_rate[:, positions], (1, 0, 2))
    obs_windows = jnp.transpose(padded_obs[:, positions], (1, 0, 2))
    state_blocks = jnp.transpose(stacked.reshape(3, ensemble, blocks_total, BLOCK), (2, 0, 1, 3))
    results = lax.map(lambda items: analyse(items[0], items[1], items[2]), (state_blocks, rate_windows, obs_windows))
    return jnp.transpose(results, (1, 2, 0, 3)).reshape(3, ensemble, N_PATCH, PATCH_DEV)
```

```python
import jax
import jax.numpy as jnp
from jax import lax
from jax.experimental import pallas as pl
from jax.experimental.pallas import tpu as pltpu
from jax.sharding import PartitionSpec as P

STEPS = 2
NEWTON = 4
NS_ITERS = 6
MARGIN = 8
F32, BF16 = jnp.float32, jnp.bfloat16


time_step = 0.25
plate_rate = 1.0

def from_everyone(x, axis):
    copies = jnp.broadcast_to(x, (lax.axis_size(axis), *x.shape))
    return lax.all_to_all(copies, axis, split_axis=0, concat_axis=0, tiled=True)


def joined_along(blocks, dim):
    blocks = jnp.moveaxis(blocks, 0, dim)
    dims = blocks.shape
    return blocks.reshape(*dims[:dim], dims[dim] * dims[dim + 1], *dims[dim + 2 :])


def gather_directly(x, axis, dim):
    blocks = from_everyone(x, axis)
    return joined_along(blocks, dim)


def inverse_sinh(value):
    magnitude = jnp.abs(value)
    result = jnp.log(magnitude + jnp.sqrt(magnitude * magnitude + 1.0))
    return jnp.where(value < 0, -result, result)


def slip_rate(stress, state_log, guess, friction_rate, damping):
    factor = 0.5 * jnp.exp(state_log / friction_rate)
    velocity = guess
    for _ in range(NEWTON):
        scaled = factor * velocity
        residual = friction_rate * inverse_sinh(scaled) + damping * velocity - stress
        derivative = friction_rate * factor / jnp.sqrt(1.0 + scaled * scaled) + damping
        velocity = velocity - residual / derivative
    return velocity


def split(x):
    high = x.astype(BF16)
    return high, (x - high.astype(F32)).astype(BF16)


def product(rows, blocks):
    row_high, row_low = split(rows)
    block_high, block_low = blocks
    count = rows.shape[0]
    both = jnp.dot(jnp.concatenate([row_high, row_low], 0), block_high, preferred_element_type=F32)
    rest = jnp.dot(row_high, block_low, preferred_element_type=F32)
    return both[:count] + (both[count:] + rest)


def product_nt(a, b):
    dims = (((1,), (1,)), ((), ()))
    ah, al = split(a)
    bh, bl = split(b)
    count = a.shape[0]
    both = lax.dot_general(jnp.concatenate([ah, al], 0), bh, dims, preferred_element_type=F32)
    rest = lax.dot_general(ah, bl, dims, preferred_element_type=F32)
    return both[:count] + (both[count:] + rest)


def tables(obs_window, sub_block, per_group):
    window = sub_block + 2 * MARGIN
    distance = jnp.abs(
        jnp.arange(sub_block, dtype=jnp.int32)[:, None]
        + MARGIN
        - jnp.arange(window, dtype=jnp.int32)[None, :]
    ).astype(F32)
    taper = jnp.where(distance <= MARGIN, jnp.exp(-0.5 * (distance / MARGIN) ** 2), 0.0)
    weights = taper * obs_window[1][None, :]
    groups = sub_block // per_group
    lanes = per_group * window
    w = weights.reshape(groups, per_group, window)
    root = jnp.sqrt(w)
    across = jnp.broadcast_to(
        jnp.transpose(root, (0, 2, 1))[:, :, :, None], (groups, window, per_group, window)
    ).reshape(groups, window, lanes)
    along = root.reshape(groups, 1, lanes)
    obs = jnp.tile(obs_window[0], per_group)[None, None, :]
    obs = jnp.broadcast_to(obs, (groups, 1, lanes))
    filler = jnp.zeros((groups, 6, lanes), F32)
    return jnp.concatenate([across * along, across * across, along, obs, filler], axis=1)


def analysis_kernel(got_ref, table_ref, out_ref, all_ref):
    groups_m, each, width = got_ref.shape
    ensemble = groups_m * each
    sub_block = (width - 2 * MARGIN) // 3
    window = sub_block + 2 * MARGIN
    halves, _, lanes = table_ref.shape
    count = lanes // window
    for g in range(groups_m):
        all_ref[g * each : (g + 1) * each, :] = got_ref[g]
    values = all_ref[...]
    mean = jnp.mean(values, axis=0, keepdims=True)
    anomaly = values - mean
    y = anomaly[:, 2 * sub_block :]
    y_tiled = jnp.concatenate([y] * count, axis=1)
    mean_tiled = jnp.concatenate([mean[:, 2 * sub_block :]] * count, axis=1)
    starts = (0, sub_block, 2 * sub_block + MARGIN)
    pieces = [y]
    for h in range(halves):
        pieces += [anomaly[:, s + h * count : s + (h + 1) * count] for s in starts]
    turned = jnp.transpose(jnp.concatenate(pieces, axis=1))
    grams = product(turned, split(y_tiled))
    gram = grams[:window]
    row = lax.broadcasted_iota(jnp.int32, (window, lanes), 0)
    lane = lax.broadcasted_iota(jnp.int32, (window, lanes), 1)
    eye = jnp.where(row == lane % window, 1.0, 0.0).astype(F32)
    block_row = lax.broadcasted_iota(jnp.int32, (lanes, lanes), 0) // window
    block_lane = lax.broadcasted_iota(jnp.int32, (lanes, lanes), 1) // window
    on_block = block_row == block_lane
    diag = jnp.sum(
        jnp.where(
            lax.broadcasted_iota(jnp.int32, (window, window), 0)
            == lax.broadcasted_iota(jnp.int32, (window, window), 1),
            gram[:, :window],
            0.0,
        ),
        axis=1,
        keepdims=True,
    )
    vrows = 3 * count
    own = lax.broadcasted_iota(jnp.int32, (vrows, lanes), 0) % count == (
        lax.broadcasted_iota(jnp.int32, (vrows, lanes), 1) // window
    )
    first = own & (lax.broadcasted_iota(jnp.int32, (vrows, lanes), 1) % window == 0)

    def blocks(x):
        return tuple(
            jnp.where(on_block, jnp.concatenate([part] * count, 0), jnp.zeros((), BF16))
            for part in split(x)
        )

    free = ensemble - 1.0
    state = []
    for h in range(halves):
        table = table_ref[h]
        cross = gram * table[:window]
        scale = free + jnp.sum(diag * table[window : 2 * window], axis=0, keepdims=True)
        inv = 1.0 / scale
        base = cross * inv
        root = table[2 * window : 2 * window + 1]
        obs = table[2 * window + 1 : 2 * window + 2]
        q = jnp.where(own, grams[window + h * vrows : window + (h + 1) * vrows] * root, 0.0)
        drive = (obs - mean_tiled) * root
        r = free * inv
        state.append(dict(base=base, inv=inv, root=root, q=q, drive=drive, r=r))
    for s in state:
        base, r = s["base"], s["r"]
        full_r = r * eye + base
        g = 1.5 - 0.5 * r
        gain = g * eye - 0.5 * base
        s["S"] = gain - 0.5 * r * eye
        s["T"] = -0.5 * eye
        s["r"], s["z"] = r * g, g
        s["fz"] = gain
        s["fr"] = product(full_r, blocks(gain))
    for it in range(1, NS_ITERS):
        last = it == NS_ITERS - 1
        for s in state:
            rb = blocks(s["fr"])
            if it == 1:
                zr, tr = product(s["fz"], rb), -0.5 * s["fr"]
            else:
                both = product(jnp.concatenate([s["fz"], s["T"]], 0), rb)
                zr, tr = both[:window], both[window:]
            s["G"] = 1.5 * eye - 0.5 * zr
            s["H"] = -0.5 * (s["z"] * s["S"] + tr)
        for s in state:
            g = 1.5 - 0.5 * s["z"] * s["r"]
            s["T"] = g * s["T"] + product(s["H"], blocks(s["fz"]))
            rows = [s["fz"]] if last else [s["fz"], s["fr"], s["S"]]
            both = product(jnp.concatenate(rows, 0), blocks(s["G"]))
            s["fz"] = both[:window]
            if not last:
                s["fr"] = both[window : 2 * window]
                s["S"] = both[2 * window :] + s["r"] * s["H"]
            s["r"], s["z"] = s["r"] * g, s["z"] * g
    ones = jnp.ones((ensemble, lanes), F32)
    results = []
    for h, s in enumerate(state):
        u = product(s["q"], blocks(s["T"])) * (s["root"] * s["inv"])
        pad = jnp.zeros((7, lanes), F32)
        rows = jnp.concatenate([s["q"], s["drive"], pad], 0)
        through = product(rows, blocks(s["fz"]))
        factor = jnp.sqrt(free * s["inv"])
        shift = through[:vrows] * (through[vrows : vrows + 1] * s["inv"])
        right = jnp.concatenate([u * factor, shift], axis=1)
        left = jnp.concatenate([y_tiled, ones], axis=1)
        part = product_nt(left, right)
        keep = jnp.where(first, s["z"] * factor, 0.0)
        weight = product_nt(jnp.ones((8, lanes), F32), keep)[:1]
        for v in range(3):
            c = slice(starts[v] + h * count, starts[v] + (h + 1) * count)
            d = slice(v * count, (v + 1) * count)
            out_ref[v, :, h * count : (h + 1) * count] = (
                mean[:, c] + anomaly[:, c] * weight[:, d] + part[:, d]
            )


def analyse(received, obs_window):
    groups_m, each, width = received.shape
    ensemble = groups_m * each
    sub_block = (width - 2 * MARGIN) // 3
    per_group = 256 // (sub_block + 2 * MARGIN)
    table = tables(obs_window, sub_block, per_group)
    return pl.pallas_call(
        analysis_kernel,
        out_shape=jax.ShapeDtypeStruct((3, ensemble, sub_block), F32),
        in_specs=[pl.BlockSpec(memory_space=pltpu.VMEM)] * 2,
        out_specs=pl.BlockSpec(memory_space=pltpu.VMEM),
        scratch_shapes=[pltpu.VMEM((ensemble, width), F32)],
        compiler_params=pltpu.CompilerParams(vmem_limit_bytes=32 * 1024 * 1024),
    )(received, table)


def from_neighbours(block, dim):
    count = lax.axis_size("patch")
    size = block.shape[dim]
    tail = lax.slice_in_dim(block, size - MARGIN, size, axis=dim)
    front = lax.slice_in_dim(block, 0, MARGIN, axis=dim)
    before = lax.ppermute(tail, "patch", [(i, i + 1) for i in range(count - 1)])
    after = lax.ppermute(front, "patch", [(i + 1, i) for i in range(count - 1)])
    return jnp.concatenate([before, after], axis=dim)


def body(
    kernel_rows,
    row_scale,
    self_stiffness,
    base_stress,
    friction_rate,
    damping,
    deficit_start,
    state_start,
    obs_rate,
    obs_precision,
):
    groups = lax.axis_size("member")
    own_rows = kernel_rows.shape[0]
    members = deficit_start.shape[0]
    sub_block = own_rows // groups
    params = jnp.stack(
        [row_scale, self_stiffness, base_stress, friction_rate, damping, obs_rate, obs_precision]
    )
    rim_rows = from_neighbours(kernel_rows, 0)
    rim_params = from_neighbours(params, 1)

    def summed(gathered, rows):
        return lax.dot_general(
            gathered, rows, (((1,), (1,)), ((), ())), preferred_element_type=jnp.float32
        )

    def gather(deficit):
        return gather_directly(deficit.astype(jnp.bfloat16), "patch", 1)

    def coupling(deficit):
        total = summed(gather(deficit), kernel_rows)
        return base_stress + self_stiffness * deficit + row_scale * total

    def tendency(deficit, state_log, guess):
        velocity = slip_rate(coupling(deficit), state_log, guess, friction_rate, damping)
        return (plate_rate - velocity, jnp.exp(-state_log) - jnp.abs(velocity), velocity)

    deficit = deficit_start
    state_log = state_start
    velocity = jnp.zeros_like(deficit_start)
    for _ in range(STEPS):
        deficit_zero, state_zero = (deficit, state_log)
        change, state_change, velocity = tendency(deficit_zero, state_zero, velocity)
        deficit_one = deficit_zero + time_step * change
        state_one = state_zero + time_step * state_change
        change, state_change, velocity = tendency(deficit_one, state_one, velocity)
        deficit_two = 0.75 * deficit_zero + 0.25 * (deficit_one + time_step * change)
        state_two = 0.75 * state_zero + 0.25 * (state_one + time_step * state_change)
        change, state_change, velocity = tendency(deficit_two, state_two, velocity)
        deficit = deficit_zero / 3.0 + 2.0 / 3.0 * (deficit_two + time_step * change)
        state_log = state_zero / 3.0 + 2.0 / 3.0 * (state_two + time_step * state_change)
    gathered = gather(deficit)
    rim = from_neighbours(jnp.stack([deficit, state_log, velocity]), 2)
    rim_scale, rim_stiffness, rim_base, rim_friction, rim_damping = rim_params[:5]
    stress = base_stress + self_stiffness * deficit + row_scale * summed(gathered, kernel_rows)
    forecast = slip_rate(stress, state_log, velocity, friction_rate, damping)
    rim_stress = rim_base + rim_stiffness * rim[0] + rim_scale * summed(gathered, rim_rows)
    there = rim_damping > 0
    rim_forecast = slip_rate(
        rim_stress,
        rim[1],
        rim[2],
        jnp.where(there, rim_friction, 1.0),
        jnp.where(there, rim_damping, 1.0),
    )
    rim_forecast = jnp.where(there, rim_forecast, 0.0)
    wide = jnp.concatenate([rim_forecast[:, :MARGIN], forecast, rim_forecast[:, MARGIN:]], axis=1)
    parts = [
        x.reshape(members, groups, sub_block)
        for x in (deficit, state_log, wide[:, :own_rows], wide[:, 2 * MARGIN :])
    ]
    sent = jnp.transpose(jnp.concatenate(parts, axis=2), (1, 0, 2))
    received = lax.all_to_all(sent, "member", split_axis=0, concat_axis=0, tiled=True)
    group_index = lax.axis_index("member")
    observed = jnp.concatenate(
        [rim_params[5:, :MARGIN], params[5:], rim_params[5:, MARGIN:]], axis=1
    )
    obs_window = lax.dynamic_slice_in_dim(
        observed, group_index * sub_block, sub_block + 2 * MARGIN, 1
    )
    analysis = analyse(received, obs_window)
    return analysis[:, :, None, :]


def solution(mesh):
    return jax.shard_map(
        body,
        mesh=mesh,
        in_specs=(
            P("patch", None),
            P("patch"),
            P("patch"),
            P("patch"),
            P("patch"),
            P("patch"),
            P("member", "patch"),
            P("member", "patch"),
            P("patch"),
            P("patch"),
        ),
        out_specs=P(None, None, "patch", "member"),
        check_vma=False,
    )
```

```python
import jax
import jax.numpy as jnp
from jax import lax
from jax.experimental import pallas as pl
from jax.experimental.pallas import tpu as pltpu
from jax.sharding import PartitionSpec as P

STEPS = 2
NEWTON = 4
NS_ITERS = 6
MARGIN = 8
F32, BF16 = jnp.float32, jnp.bfloat16
PARTS = (3, 2, 2, 3, 2, 3)


time_step = 0.25
plate_rate = 1.0

def from_everyone(x, axis):
    copies = jnp.broadcast_to(x, (lax.axis_size(axis), *x.shape))
    return lax.all_to_all(copies, axis, split_axis=0, concat_axis=0, tiled=True)


def joined_along(blocks, dim):
    blocks = jnp.moveaxis(blocks, 0, dim)
    dims = blocks.shape
    return blocks.reshape(*dims[:dim], dims[dim] * dims[dim + 1], *dims[dim + 2 :])


def gather_directly(x, axis, dim):
    blocks = from_everyone(x, axis)
    return joined_along(blocks, dim)


def inverse_sinh(value):
    magnitude = jnp.abs(value)
    result = jnp.log(magnitude + jnp.sqrt(magnitude * magnitude + 1.0))
    return jnp.where(value < 0, -result, result)


def slip_rate(stress, state_log, guess, friction_rate, damping):
    factor = 0.5 * jnp.exp(state_log / friction_rate)
    velocity = guess
    for _ in range(NEWTON):
        scaled = factor * velocity
        residual = friction_rate * inverse_sinh(scaled) + damping * velocity - stress
        derivative = friction_rate * factor / jnp.sqrt(1.0 + scaled * scaled) + damping
        velocity = velocity - residual / derivative
    return velocity


def split(x, parts=2):
    pieces = []
    for _ in range(parts):
        pieces.append(x.astype(BF16))
        x = x - pieces[-1].astype(F32)
    return pieces


def product(rows, right, dims=(((1,), (0,)), ((), ()))):
    left = split(rows, len(right))
    count = rows.shape[0]
    total = None
    for i, piece in reversed(list(enumerate(right))):
        stacked = jnp.concatenate(left[: len(right) - i], 0)
        sums = lax.dot_general(stacked, piece, dims, preferred_element_type=F32)
        for j in reversed(range(len(right) - i)):
            term = sums[j * count : (j + 1) * count]
            total = term if total is None else total + term
    return total


def tables(obs_window, sub_block, per_group):
    window = sub_block + 2 * MARGIN
    distance = jnp.abs(
        jnp.arange(sub_block, dtype=jnp.int32)[:, None]
        + MARGIN
        - jnp.arange(window, dtype=jnp.int32)[None, :]
    ).astype(F32)
    taper = jnp.where(distance <= MARGIN, jnp.exp(-0.5 * (distance / MARGIN) ** 2), 0.0)
    weights = taper * obs_window[1][None, :]
    groups = sub_block // per_group
    lanes = per_group * window
    w = weights.reshape(groups, per_group, window)
    root = jnp.sqrt(w)
    across = jnp.broadcast_to(
        jnp.transpose(root, (0, 2, 1))[:, :, :, None], (groups, window, per_group, window)
    ).reshape(groups, window, lanes)
    along = root.reshape(groups, 1, lanes)
    obs = jnp.tile(obs_window[0], per_group)[None, None, :]
    obs = jnp.broadcast_to(obs, (groups, 1, lanes))
    filler = jnp.zeros((groups, 6, lanes), F32)
    return jnp.concatenate([across * along, across * across, along, obs, filler], axis=1)


def pack_kernel(deficit_ref, state_ref, rate_ref, rim_ref, out_ref):
    count, rows, width = out_ref.shape
    members, own = rate_ref.shape
    sub_block = own // count
    half = members // 2
    rim = rim_ref[...]
    wide = jnp.concatenate([rim[:, :MARGIN], rate_ref[...], rim[:, MARGIN:]], axis=1)
    out_ref[...] = jnp.zeros(out_ref.shape, F32)
    for g in range(count):
        here = slice(g * sub_block, (g + 1) * sub_block)
        piece = jnp.concatenate(
            [
                deficit_ref[:, here],
                state_ref[:, here],
                wide[:, g * sub_block : (g + 1) * sub_block + 2 * MARGIN],
            ],
            axis=1,
        )
        out_ref[g, :half, :] = jnp.concatenate([piece[:half], piece[half:]], axis=1)


def analysis_kernel(got_ref, table_ref, out_ref, all_ref):
    groups_m, _, width = got_ref.shape
    width = width // 2
    ensemble = all_ref.shape[0]
    half = ensemble // groups_m // 2
    sub_block = (width - 2 * MARGIN) // 3
    window = sub_block + 2 * MARGIN
    halves, _, lanes = table_ref.shape
    count = lanes // window
    for g in range(groups_m):
        for side in range(2):
            at = (2 * g + side) * half
            all_ref[at : at + half, :] = got_ref[g, :half, side * width : (side + 1) * width]
    values = all_ref[...]
    rates = values[:, 2 * sub_block :]
    starts = (0, sub_block, 2 * sub_block + MARGIN)
    pieces = [rates]
    for h in range(halves):
        pieces += [values[:, s + h * count : s + (h + 1) * count] for s in starts]
    turned = jnp.transpose(jnp.concatenate(pieces, axis=1))
    turned_mean = jnp.mean(turned, axis=1, keepdims=True)
    turned = turned - turned_mean
    rates_tiled = jnp.concatenate([rates] * count, axis=1)
    mean_tiled = jnp.mean(rates_tiled, axis=0, keepdims=True)
    y = split(rates_tiled - mean_tiled, 3)
    grams = product(turned, y)
    gram = grams[:window]
    row = lax.broadcasted_iota(jnp.int32, (window, lanes), 0)
    lane = lax.broadcasted_iota(jnp.int32, (window, lanes), 1)
    eye = jnp.where(row == lane % window, 1.0, 0.0).astype(F32)
    block_row = lax.broadcasted_iota(jnp.int32, (lanes, lanes), 0) // window
    block_lane = lax.broadcasted_iota(jnp.int32, (lanes, lanes), 1) // window
    on_block = block_row == block_lane
    diag = jnp.sum(
        jnp.where(
            lax.broadcasted_iota(jnp.int32, (window, window), 0)
            == lax.broadcasted_iota(jnp.int32, (window, window), 1),
            gram[:, :window],
            0.0,
        ),
        axis=1,
        keepdims=True,
    )
    vrows = 3 * count
    own = lax.broadcasted_iota(jnp.int32, (vrows, lanes), 0) % count == (
        lax.broadcasted_iota(jnp.int32, (vrows, lanes), 1) // window
    )
    first = own & (lax.broadcasted_iota(jnp.int32, (vrows, lanes), 1) % window == 0)

    def blocks(x, parts=2):
        return tuple(
            jnp.where(on_block, jnp.concatenate([part] * count, 0), jnp.zeros((), BF16))
            for part in split(x, parts)
        )

    free = ensemble - 1.0
    state = []
    for h in range(halves):
        table = table_ref[h]
        cross = gram * table[:window]
        scale = free + jnp.sum(diag * table[window : 2 * window], axis=0, keepdims=True)
        inv = 1.0 / scale
        base = cross * inv
        root = table[2 * window : 2 * window + 1]
        obs = table[2 * window + 1 : 2 * window + 2]
        q = jnp.where(own, grams[window + h * vrows : window + (h + 1) * vrows] * root, 0.0)
        drive = (obs - mean_tiled) * root
        r = free * inv
        state.append(dict(base=base, inv=inv, root=root, q=q, drive=drive, r=r))
    for s in state:
        base, r = s["base"], s["r"]
        full_r = r * eye + base
        g = 1.5 - 0.5 * r
        gain = g * eye - 0.5 * base
        s["S"] = gain - 0.5 * r * eye
        s["T"] = -0.5 * eye
        s["r"], s["z"] = r * g, g
        s["fz"] = gain
        s["fr"] = product(full_r, blocks(gain, PARTS[0]))
    for it in range(1, NS_ITERS):
        last = it == NS_ITERS - 1
        for s in state:
            rb = blocks(s["fr"], PARTS[1])
            if it == 1:
                zr, tr = product(s["fz"], rb), -0.5 * s["fr"]
            else:
                both = product(jnp.concatenate([s["fz"], s["T"]], 0), rb)
                zr, tr = both[:window], both[window:]
            s["G"] = 1.5 * eye - 0.5 * zr
            s["H"] = -0.5 * (s["z"] * s["S"] + tr)
        for s in state:
            g = 1.5 - 0.5 * s["z"] * s["r"]
            s["T"] = g * s["T"] + product(s["H"], blocks(s["fz"], PARTS[2]))
            rows = [s["fz"]] if last else [s["fz"], s["fr"], s["S"]]
            both = product(jnp.concatenate(rows, 0), blocks(s["G"], PARTS[3]))
            s["fz"] = both[:window]
            if not last:
                s["fr"] = both[window : 2 * window]
                s["S"] = both[2 * window :] + s["r"] * s["H"]
            s["r"], s["z"] = s["r"] * g, s["z"] * g
    for h, s in enumerate(state):
        here = slice(window + h * vrows, window + (h + 1) * vrows)
        u = product(s["q"], blocks(s["T"], PARTS[4])) * (s["root"] * s["inv"])
        rows = jnp.concatenate([s["q"], s["drive"], jnp.zeros((7, lanes), F32)], 0)
        through = product(rows, blocks(s["fz"], PARTS[5]))
        factor = jnp.sqrt(free * s["inv"])
        shift = through[:vrows] * (through[vrows : vrows + 1] * s["inv"])
        shift = jnp.sum(shift, axis=1, keepdims=True)
        keep = jnp.sum(jnp.where(first, s["z"] * factor, 0.0), axis=1, keepdims=True)
        spread = product(u * factor, y, (((1,), (1,)), ((), ())))
        result = turned_mean[here] + shift + keep * turned[here] + spread
        for v in range(3):
            out_ref[v, h * count : (h + 1) * count, :] = result[v * count : (v + 1) * count]


def pack(deficit, state_log, rates, rim, count):
    members, own = rates.shape
    width = 2 * (3 * (own // count) + 2 * MARGIN)
    rows = -(-members // 4) * 2
    return pl.pallas_call(
        pack_kernel,
        out_shape=jax.ShapeDtypeStruct((count, rows, width), F32),
        in_specs=[pl.BlockSpec(memory_space=pltpu.VMEM)] * 4,
        out_specs=pl.BlockSpec(memory_space=pltpu.VMEM),
        compiler_params=pltpu.CompilerParams(vmem_limit_bytes=8 * 1024 * 1024),
    )(deficit, state_log, rates, rim)


def analyse(received, table, ensemble):
    width = received.shape[2] // 2
    sub_block = (width - 2 * MARGIN) // 3
    return pl.pallas_call(
        analysis_kernel,
        out_shape=jax.ShapeDtypeStruct((3, sub_block, ensemble), F32),
        in_specs=[pl.BlockSpec(memory_space=pltpu.VMEM)] * 2,
        out_specs=pl.BlockSpec(memory_space=pltpu.VMEM),
        scratch_shapes=[pltpu.VMEM((ensemble, width), F32)],
        compiler_params=pltpu.CompilerParams(vmem_limit_bytes=16 * 1024 * 1024),
    )(received, table)


def from_neighbours(block, dim):
    count = lax.axis_size("patch")
    size = block.shape[dim]
    tail = lax.slice_in_dim(block, size - MARGIN, size, axis=dim)
    front = lax.slice_in_dim(block, 0, MARGIN, axis=dim)
    before = lax.ppermute(tail, "patch", [(i, i + 1) for i in range(count - 1)])
    after = lax.ppermute(front, "patch", [(i + 1, i) for i in range(count - 1)])
    return jnp.concatenate([before, after], axis=dim)


def body(
    kernel_rows,
    row_scale,
    self_stiffness,
    base_stress,
    friction_rate,
    damping,
    deficit_start,
    state_start,
    obs_rate,
    obs_precision,
):
    groups = lax.axis_size("member")
    own_rows = kernel_rows.shape[0]
    members = deficit_start.shape[0]
    sub_block = own_rows // groups
    params = jnp.stack(
        [row_scale, self_stiffness, base_stress, friction_rate, damping, obs_rate, obs_precision]
    )
    rim_rows = from_neighbours(kernel_rows, 0)
    rim_params = from_neighbours(params, 1)

    group_index = lax.axis_index("member")
    observed = jnp.concatenate(
        [rim_params[5:, :MARGIN], params[5:], rim_params[5:, MARGIN:]], axis=1
    )
    obs_window = lax.dynamic_slice_in_dim(
        observed, group_index * sub_block, sub_block + 2 * MARGIN, 1
    )
    table = tables(obs_window, sub_block, 256 // (sub_block + 2 * MARGIN))
    rim_scale, rim_stiffness, rim_base, rim_friction, rim_damping = rim_params[:5]
    there = rim_damping > 0
    rim_friction = jnp.where(there, rim_friction, 1.0)
    rim_damping = jnp.where(there, rim_damping, 1.0)
    rim_given = (
        rim_rows,
        rim_scale,
        rim_stiffness,
        rim_base,
        rim_friction,
        rim_damping,
        there.astype(jnp.float32),
    )

    def summed(gathered, rows):
        return lax.dot_general(
            gathered, rows, (((1,), (1,)), ((), ())), preferred_element_type=jnp.float32
        )

    def gather(deficit):
        return gather_directly(deficit.astype(jnp.bfloat16), "patch", 1)

    def tendency(gathered, deficit, state_log, guess):
        total = summed(gathered, kernel_rows)
        stress = base_stress + self_stiffness * deficit + row_scale * total
        velocity = slip_rate(stress, state_log, guess, friction_rate, damping)
        return (plate_rate - velocity, jnp.exp(-state_log) - jnp.abs(velocity), velocity)

    deficit = deficit_start
    state_log = state_start
    velocity = jnp.zeros_like(deficit_start)
    for step in range(STEPS):
        deficit_zero, state_zero = (deficit, state_log)
        change, state_change, velocity = tendency(
            gather(deficit_zero), deficit_zero, state_zero, velocity
        )
        deficit_one = deficit_zero + time_step * change
        state_one = state_zero + time_step * state_change
        rounded = deficit_one.astype(jnp.bfloat16)
        if step == 0:
            rounded, table, rim_given = lax.optimization_barrier((rounded, table, rim_given))
        change, state_change, velocity = tendency(
            gather_directly(rounded, "patch", 1), deficit_one, state_one, velocity
        )
        deficit_two = 0.75 * deficit_zero + 0.25 * (deficit_one + time_step * change)
        state_two = 0.75 * state_zero + 0.25 * (state_one + time_step * state_change)
        change, state_change, velocity = tendency(
            gather(deficit_two), deficit_two, state_two, velocity
        )
        deficit = deficit_zero / 3.0 + 2.0 / 3.0 * (deficit_two + time_step * change)
        state_log = state_zero / 3.0 + 2.0 / 3.0 * (state_two + time_step * state_change)
    rounded, rim_given = lax.optimization_barrier((deficit.astype(jnp.bfloat16), rim_given))
    gathered = gather_directly(rounded, "patch", 1)
    rim = from_neighbours(jnp.stack([deficit, state_log, velocity]), 2)
    rim_rows, rim_scale, rim_stiffness, rim_base, rim_friction, rim_damping, there = rim_given
    stress = base_stress + self_stiffness * deficit + row_scale * summed(gathered, kernel_rows)
    forecast = slip_rate(stress, state_log, velocity, friction_rate, damping)
    rim_stress = rim_base + rim_stiffness * rim[0] + rim_scale * summed(gathered, rim_rows)
    rim_forecast = slip_rate(rim_stress, rim[1], rim[2], rim_friction, rim_damping)
    rim_forecast = jnp.where(there > 0, rim_forecast, 0.0)
    sent = pack(deficit, state_log, forecast, rim_forecast, groups)
    received = lax.all_to_all(sent, "member", split_axis=0, concat_axis=0, tiled=True)
    analysis = jnp.transpose(analyse(received, table, members * groups), (0, 2, 1))
    return analysis[:, :, None, :]


def solution(mesh):
    return jax.shard_map(
        body,
        mesh=mesh,
        in_specs=(
            P("patch", None),
            P("patch"),
            P("patch"),
            P("patch"),
            P("patch"),
            P("patch"),
            P("member", "patch"),
            P("member", "patch"),
            P("patch"),
            P("patch"),
        ),
        out_specs=P(None, None, "patch", "member"),
        check_vma=False,
    )
```

```python
import functools
import jax
import numpy as np
import jax.numpy as jnp
from jax import lax
from jax.experimental import pallas as pl
from jax.experimental.pallas import tpu as pltpu
from jax.sharding import PartitionSpec as P

STEPS = 2
NEWTON = 4
NS_ITERS = 6
MARGIN = 8
F32, BF16 = jnp.float32, jnp.bfloat16
PARTS = (3, 2, 2, 3, 2, 3)
LANES = 128


time_step = 0.25
plate_rate = 1.0

def from_everyone(x, axis):
    copies = jnp.broadcast_to(x, (lax.axis_size(axis), *x.shape))
    return lax.all_to_all(copies, axis, split_axis=0, concat_axis=0, tiled=True)


def joined_along(blocks, dim):
    blocks = jnp.moveaxis(blocks, 0, dim)
    dims = blocks.shape
    return blocks.reshape(*dims[:dim], dims[dim] * dims[dim + 1], *dims[dim + 2 :])


def inverse_sinh(value):
    magnitude = jnp.abs(value)
    result = jnp.log(magnitude + jnp.sqrt(magnitude * magnitude + 1.0))
    return jnp.where(value < 0, -result, result)


def slip_rate(stress, state_log, guess, friction_rate, damping):
    factor = 0.5 * jnp.exp(state_log / friction_rate)
    velocity = guess
    for _ in range(NEWTON):
        scaled = factor * velocity
        residual = friction_rate * inverse_sinh(scaled) + damping * velocity - stress
        derivative = friction_rate * factor / jnp.sqrt(1.0 + scaled * scaled) + damping
        velocity = velocity - residual / derivative
    return velocity


def split(x, parts=2):
    pieces = []
    for _ in range(parts):
        pieces.append(x.astype(BF16))
        x = x - pieces[-1].astype(F32)
    return pieces


def product(rows, right, dims=(((1,), (0,)), ((), ()))):
    left = split(rows, len(right))
    count = rows.shape[0]
    total = None
    for i, piece in reversed(list(enumerate(right))):
        stacked = jnp.concatenate(left[: len(right) - i], 0)
        sums = lax.dot_general(stacked, piece, dims, preferred_element_type=F32)
        for j in reversed(range(len(right) - i)):
            term = sums[j * count : (j + 1) * count]
            total = term if total is None else total + term
    return total


def tables(obs_window, sub_block, group_index, groups):
    window = sub_block + 2 * MARGIN
    together = LANES // window
    sets = sub_block // together
    distance = np.abs(np.arange(sub_block)[:, None] + MARGIN - np.arange(window)[None, :])
    taper = np.where(distance <= MARGIN, np.exp(-0.5 * (distance / MARGIN) ** 2), 0.0)
    taper = taper.reshape(sets, together, window)
    across = np.broadcast_to(
        np.transpose(taper, (0, 2, 1))[:, :, :, None], (sets, window, together, window)
    ).reshape(sets, window, LANES)
    along = taper.reshape(sets, 1, LANES)
    root = np.sqrt(across * along).astype(np.float32)
    root_along = np.sqrt(along).astype(np.float32)
    across = across.astype(np.float32)
    precision = obs_window[1]
    root_precision = jnp.sqrt(precision)
    root_tiled = jnp.tile(root_precision, together)[None, None, :]
    lane = np.arange(LANES) % window
    from_across = jnp.where(
        group_index == 0,
        lane < MARGIN,
        jnp.where(group_index == groups - 1, lane >= window - MARGIN, False),
    )
    rows = jnp.stack([jnp.tile(obs_window[0], together), from_across.astype(F32)])
    return jnp.concatenate(
        [
            root * root_precision[None, :, None] * root_tiled,
            across * precision[None, :, None],
            root_along * root_tiled,
            jnp.broadcast_to(rows[None], (sets, 2, LANES)),
            jnp.zeros((sets, 5, LANES), F32),
        ],
        axis=1,
    )


def pack_kernel(members, deficit_ref, state_ref, rate_ref, out_ref):
    count, rows, width = out_ref.shape
    own = rate_ref.shape[1]
    sub_block = own // count
    half = members // 2
    rim = jnp.zeros((rate_ref.shape[0], MARGIN), F32)
    wide = jnp.concatenate([rim, rate_ref[...], rim], axis=1)
    out_ref[...] = jnp.zeros(out_ref.shape, F32)
    for g in range(count):
        here = slice(g * sub_block, (g + 1) * sub_block)
        piece = jnp.concatenate(
            [
                deficit_ref[:, here],
                state_ref[:, here],
                wide[:, g * sub_block : (g + 1) * sub_block + 2 * MARGIN],
            ],
            axis=1,
        )
        out_ref[g, :half, :] = jnp.concatenate([piece[:half], piece[half:members]], axis=1)


def analysis_kernel(got_ref, across_ref, table_ref, out_ref, all_ref):
    groups_m, _, width = got_ref.shape
    width = width // 2
    ensemble = all_ref.shape[1]
    half = ensemble // groups_m // 2
    sub_block = (width - 2 * MARGIN) // 3
    window = sub_block + 2 * MARGIN
    halves, _, lanes = table_ref.shape
    count = lanes // window
    for g in range(groups_m):
        for side in range(2):
            at = (2 * g + side) * half
            part = slice(side * width, (side + 1) * width)
            all_ref[0, at : at + half, :] = got_ref[g, :half, part]
            all_ref[1, at : at + half, :] = across_ref[g, :half, part]
    values = all_ref[0]
    rates = values[:, 2 * sub_block :]
    beyond = all_ref[1][:, 2 * sub_block :]
    beyond = jnp.concatenate([beyond[:, sub_block:], beyond[:, :sub_block]], axis=1)
    edge = table_ref[0, 2 * window + 2 : 2 * window + 3, :window]
    rates = jnp.where(edge > 0, beyond, rates)
    starts = (0, sub_block, 2 * sub_block + MARGIN)
    pieces = [rates]
    for h in range(halves):
        pieces += [values[:, s + h * count : s + (h + 1) * count] for s in starts]
    turned = jnp.transpose(jnp.concatenate(pieces, axis=1))
    turned_mean = jnp.mean(turned, axis=1, keepdims=True)
    turned = turned - turned_mean
    rates_tiled = jnp.concatenate([rates] * count, axis=1)
    mean_tiled = jnp.mean(rates_tiled, axis=0, keepdims=True)
    y = split(rates_tiled - mean_tiled, 3)
    grams = product(turned, y)
    gram = grams[:window]
    row = lax.broadcasted_iota(jnp.int32, (window, lanes), 0)
    lane = lax.broadcasted_iota(jnp.int32, (window, lanes), 1)
    eye = jnp.where(row == lane % window, 1.0, 0.0).astype(F32)
    block_row = lax.broadcasted_iota(jnp.int32, (lanes, lanes), 0) // window
    block_lane = lax.broadcasted_iota(jnp.int32, (lanes, lanes), 1) // window
    on_block = block_row == block_lane
    diag = jnp.sum(
        jnp.where(
            lax.broadcasted_iota(jnp.int32, (window, window), 0)
            == lax.broadcasted_iota(jnp.int32, (window, window), 1),
            gram[:, :window],
            0.0,
        ),
        axis=1,
        keepdims=True,
    )
    vrows = 3 * count
    own = lax.broadcasted_iota(jnp.int32, (vrows, lanes), 0) % count == (
        lax.broadcasted_iota(jnp.int32, (vrows, lanes), 1) // window
    )
    first = own & (lax.broadcasted_iota(jnp.int32, (vrows, lanes), 1) % window == 0)

    def blocks(x, parts=2):
        return tuple(
            jnp.where(on_block, jnp.concatenate([part] * count, 0), jnp.zeros((), BF16))
            for part in split(x, parts)
        )

    free = ensemble - 1.0
    state = []
    for h in range(halves):
        table = table_ref[h]
        cross = gram * table[:window]
        scale = free + jnp.sum(diag * table[window : 2 * window], axis=0, keepdims=True)
        inv = 1.0 / scale
        base = cross * inv
        root = table[2 * window : 2 * window + 1]
        obs = table[2 * window + 1 : 2 * window + 2]
        q = jnp.where(own, grams[window + h * vrows : window + (h + 1) * vrows] * root, 0.0)
        drive = (obs - mean_tiled) * root
        r = free * inv
        state.append(dict(base=base, inv=inv, root=root, q=q, drive=drive, r=r))
    for s in state:
        base, r = s["base"], s["r"]
        full_r = r * eye + base
        g = 1.5 - 0.5 * r
        gain = g * eye - 0.5 * base
        s["S"] = gain - 0.5 * r * eye
        s["T"] = -0.5 * eye
        s["r"], s["z"] = r * g, g
        s["fz"] = gain
        s["fr"] = product(full_r, blocks(gain, PARTS[0]))
    for it in range(1, NS_ITERS):
        last = it == NS_ITERS - 1
        for s in state:
            rb = blocks(s["fr"], PARTS[1])
            if it == 1:
                zr, tr = product(s["fz"], rb), -0.5 * s["fr"]
            else:
                both = product(jnp.concatenate([s["fz"], s["T"]], 0), rb)
                zr, tr = both[:window], both[window:]
            s["G"] = 1.5 * eye - 0.5 * zr
            s["H"] = -0.5 * (s["z"] * s["S"] + tr)
        for s in state:
            g = 1.5 - 0.5 * s["z"] * s["r"]
            s["T"] = g * s["T"] + product(s["H"], blocks(s["fz"], PARTS[2]))
            rows = [s["fz"]] if last else [s["fz"], s["fr"], s["S"]]
            both = product(jnp.concatenate(rows, 0), blocks(s["G"], PARTS[3]))
            s["fz"] = both[:window]
            if not last:
                s["fr"] = both[window : 2 * window]
                s["S"] = both[2 * window :] + s["r"] * s["H"]
            s["r"], s["z"] = s["r"] * g, s["z"] * g
    for h, s in enumerate(state):
        here = slice(window + h * vrows, window + (h + 1) * vrows)
        u = product(s["q"], blocks(s["T"], PARTS[4])) * (s["root"] * s["inv"])
        rows = jnp.concatenate([s["q"], s["drive"], jnp.zeros((7, lanes), F32)], 0)
        through = product(rows, blocks(s["fz"], PARTS[5]))
        factor = jnp.sqrt(free * s["inv"])
        shift = through[:vrows] * (through[vrows : vrows + 1] * s["inv"])
        shift = jnp.sum(shift, axis=1, keepdims=True)
        keep = jnp.sum(jnp.where(first, s["z"] * factor, 0.0), axis=1, keepdims=True)
        spread = product(u * factor, y, (((1,), (1,)), ((), ())))
        result = turned_mean[here] + shift + keep * turned[here] + spread
        for v in range(3):
            out_ref[v, h * count : (h + 1) * count, :] = result[v * count : (v + 1) * count]


def pack(deficit, state_log, rates, members, count):
    own = rates.shape[1]
    width = 2 * (3 * (own // count) + 2 * MARGIN)
    rows = -(-members // 4) * 2
    return pl.pallas_call(
        functools.partial(pack_kernel, members),
        out_shape=jax.ShapeDtypeStruct((count, rows, width), F32),
        in_specs=[pl.BlockSpec(memory_space=pltpu.VMEM)] * 3,
        out_specs=pl.BlockSpec(memory_space=pltpu.VMEM),
        compiler_params=pltpu.CompilerParams(vmem_limit_bytes=8 * 1024 * 1024),
    )(deficit, state_log, rates)


def analyse(received, across, table, ensemble):
    width = received.shape[2] // 2
    sub_block = (width - 2 * MARGIN) // 3
    return pl.pallas_call(
        analysis_kernel,
        out_shape=jax.ShapeDtypeStruct((3, sub_block, ensemble), F32),
        in_specs=[pl.BlockSpec(memory_space=pltpu.VMEM)] * 3,
        out_specs=pl.BlockSpec(memory_space=pltpu.VMEM),
        scratch_shapes=[pltpu.VMEM((2, ensemble, width), F32)],
        compiler_params=pltpu.CompilerParams(vmem_limit_bytes=16 * 1024 * 1024),
    )(received, across, table)


def in_pieces(x):
    pieces = []
    for _ in range(3):
        pieces.append(lax.reduce_precision(x, exponent_bits=8, mantissa_bits=7))
        x = x - pieces[-1]
    return jnp.stack(pieces).astype(BF16)


def body(
    kernel_rows,
    row_scale,
    self_stiffness,
    base_stress,
    friction_rate,
    damping,
    deficit_start,
    state_start,
    obs_rate,
    obs_precision,
):
    groups = lax.axis_size("member")
    blocks = lax.axis_size("patch")
    own_rows = kernel_rows.shape[0]
    members = deficit_start.shape[0]
    sub_block = own_rows // groups
    rows = -(-members // 8) * 8
    assert rows > members

    def gather(rounded):
        return from_everyone(rounded, "patch")

    def tendency(gathered, deficit, state_log, guess):
        velocity = section_rate(gathered, deficit, state_log, guess)
        return (plate_rate - velocity, jnp.exp(-state_log) - jnp.abs(velocity), velocity)

    def section_rate(gathered, deficit, state_log, guess):
        total = lax.dot_general(
            joined_along(gathered, 1),
            kernel_rows,
            (((1,), (1,)), ((), ())),
            preferred_element_type=F32,
        )
        stress = base_stress + self_stiffness * deficit + row_scale * total
        return slip_rate(stress, state_log, guess, friction_rate, damping)

    observed = jnp.stack([obs_rate, obs_precision])
    ends = jnp.stack([observed[:, :MARGIN], observed[:, own_rows - MARGIN :]])
    spare = in_pieces(ends).reshape(1, -1)
    spare = jnp.pad(spare, ((0, rows - members - 1), (0, own_rows - spare.shape[1])))
    full = ((0, rows - members), (0, 0))
    deficit = jnp.pad(deficit_start, full)
    state_log = jnp.pad(state_start, full)
    velocity = jnp.zeros_like(deficit)
    rounded, group_index, block_index = lax.optimization_barrier(
        (
            jnp.concatenate([deficit_start.astype(BF16), spare], axis=0),
            lax.axis_index("member"),
            lax.axis_index("patch"),
        )
    )
    first = gather(rounded)
    first, friction_rate, damping, row_scale, self_stiffness, base_stress = lax.optimization_barrier(
        (first, friction_rate, damping, row_scale, self_stiffness, base_stress)
    )
    gathered = first
    for step in range(STEPS):
        deficit_zero, state_zero = (deficit, state_log)
        if step > 0:
            gathered = gather(deficit_zero.astype(BF16))
        change, state_change, velocity = tendency(gathered, deficit_zero, state_zero, velocity)
        deficit_one = deficit_zero + time_step * change
        state_one = state_zero + time_step * state_change
        change, state_change, velocity = tendency(
            gather(deficit_one.astype(BF16)), deficit_one, state_one, velocity
        )
        deficit_two = 0.75 * deficit_zero + 0.25 * (deficit_one + time_step * change)
        state_two = 0.75 * state_zero + 0.25 * (state_one + time_step * state_change)
        change, state_change, velocity = tendency(
            gather(deficit_two.astype(BF16)), deficit_two, state_two, velocity
        )
        deficit = deficit_zero / 3.0 + 2.0 / 3.0 * (deficit_two + time_step * change)
        state_log = state_zero / 3.0 + 2.0 / 3.0 * (state_two + time_step * state_change)
    deficit, state_log, velocity = lax.optimization_barrier((deficit, state_log, velocity))
    forecast = section_rate(gather(deficit.astype(BF16)), deficit, state_log, velocity)
    sent = pack(deficit, state_log, forecast, members, groups)
    received = lax.all_to_all(sent, "member", split_axis=0, concat_axis=0, tiled=True)
    received, first, obs_rate, obs_precision, group_index, block_index = lax.optimization_barrier(
        (received, first, obs_rate, obs_precision, group_index, block_index)
    )
    observed = jnp.stack([obs_rate, obs_precision])
    spare = first[:, members]
    pairs = [((groups - 1) * blocks + p, p + 1) for p in range(blocks - 1)]
    pairs += [(b, a) for a, b in pairs]
    across = lax.ppermute(received, ("member", "patch"), pairs)

    def ends_of(block):
        row = lax.dynamic_index_in_dim(spare, jnp.clip(block, 0, blocks - 1), 0, keepdims=False)
        parts = row[: 3 * ends.size].astype(F32).reshape(3, *ends.shape)
        there = (block >= 0) & (block < blocks)
        return jnp.where(there, parts[0] + (parts[1] + parts[2]), 0.0)

    observed = jnp.concatenate(
        [ends_of(block_index - 1)[1], observed, ends_of(block_index + 1)[0]], axis=1
    )
    obs_window = lax.dynamic_slice_in_dim(
        observed, group_index * sub_block, sub_block + 2 * MARGIN, 1
    )
    table = tables(obs_window, sub_block, group_index, groups)
    analysis = jnp.transpose(analyse(received, across, table, members * groups), (0, 2, 1))
    return analysis[:, :, None, :]


def solution(mesh):
    return jax.shard_map(
        body,
        mesh=mesh,
        in_specs=(
            P("patch", None),
            P("patch"),
            P("patch"),
            P("patch"),
            P("patch"),
            P("patch"),
            P("member", "patch"),
            P("member", "patch"),
            P("patch"),
            P("patch"),
        ),
        out_specs=P(None, None, "patch", "member"),
        check_vma=False,
    )
```

```python
import functools
import jax
import numpy as np
import jax.numpy as jnp
from jax import lax
from jax.experimental import pallas as pl
from jax.experimental.pallas import tpu as pltpu
from jax.sharding import PartitionSpec as P

STEPS = 2
NEWTON = 4
NS_ITERS = 6
MARGIN = 8
F32, BF16 = jnp.float32, jnp.bfloat16
PARTS = (3, 2, 2, 3, 2, 3)
LANES = 128


time_step = 0.25
plate_rate = 1.0

def from_everyone(x, axis):
    copies = jnp.broadcast_to(x, (lax.axis_size(axis), *x.shape))
    return lax.all_to_all(copies, axis, split_axis=0, concat_axis=0, tiled=True)


def joined_along(blocks, dim):
    blocks = jnp.moveaxis(blocks, 0, dim)
    dims = blocks.shape
    return blocks.reshape(*dims[:dim], dims[dim] * dims[dim + 1], *dims[dim + 2 :])


def inverse_sinh(value):
    magnitude = jnp.abs(value)
    result = jnp.log(magnitude + jnp.sqrt(magnitude * magnitude + 1.0))
    return jnp.where(value < 0, -result, result)


def slip_rate(stress, state_log, guess, friction_rate, damping):
    factor = 0.5 * jnp.exp(state_log / friction_rate)
    velocity = guess
    for _ in range(NEWTON):
        scaled = factor * velocity
        residual = friction_rate * inverse_sinh(scaled) + damping * velocity - stress
        derivative = friction_rate * factor / jnp.sqrt(1.0 + scaled * scaled) + damping
        velocity = velocity - residual / derivative
    return velocity


def split(x, parts=2):
    pieces = []
    for _ in range(parts):
        pieces.append(x.astype(BF16))
        x = x - pieces[-1].astype(F32)
    return pieces


def product(rows, right, dims=(((1,), (0,)), ((), ()))):
    left = split(rows, len(right))
    count = rows.shape[0]
    total = None
    for i, piece in reversed(list(enumerate(right))):
        stacked = jnp.concatenate(left[: len(right) - i], 0)
        sums = lax.dot_general(stacked, piece, dims, preferred_element_type=F32)
        for j in reversed(range(len(right) - i)):
            term = sums[j * count : (j + 1) * count]
            total = term if total is None else total + term
    return total


def tables(obs_window, sub_block, group_index, groups):
    window = sub_block + 2 * MARGIN
    together = LANES // window
    sets = sub_block // together
    distance = np.abs(np.arange(sub_block)[:, None] + MARGIN - np.arange(window)[None, :])
    taper = np.where(distance <= MARGIN, np.exp(-0.5 * (distance / MARGIN) ** 2), 0.0)
    taper = taper.reshape(sets, together, window)
    across = np.broadcast_to(
        np.transpose(taper, (0, 2, 1))[:, :, :, None], (sets, window, together, window)
    ).reshape(sets, window, LANES)
    along = taper.reshape(sets, 1, LANES)
    root = np.sqrt(across * along).astype(np.float32)
    root_along = np.sqrt(along).astype(np.float32)
    across = across.astype(np.float32)
    precision = obs_window[1]
    root_precision = jnp.sqrt(precision)
    root_tiled = jnp.tile(root_precision, together)[None, None, :]
    lane = np.arange(LANES) % window
    from_across = jnp.where(
        group_index == 0,
        lane < MARGIN,
        jnp.where(group_index == groups - 1, lane >= window - MARGIN, False),
    )
    rows = jnp.stack([jnp.tile(obs_window[0], together), from_across.astype(F32)])
    return jnp.concatenate(
        [
            root * root_precision[None, :, None] * root_tiled,
            across * precision[None, :, None],
            root_along * root_tiled,
            jnp.broadcast_to(rows[None], (sets, 2, LANES)),
            jnp.zeros((sets, 5, LANES), F32),
        ],
        axis=1,
    )


def pack_kernel(members, deficit_ref, state_ref, rate_ref, out_ref):
    count, rows, width = out_ref.shape
    own = rate_ref.shape[1]
    sub_block = own // count
    half = members // 2
    rim = jnp.zeros((rate_ref.shape[0], MARGIN), F32)
    wide = jnp.concatenate([rim, rate_ref[...], rim], axis=1)
    out_ref[...] = jnp.zeros(out_ref.shape, F32)
    for g in range(count):
        here = slice(g * sub_block, (g + 1) * sub_block)
        piece = jnp.concatenate(
            [
                deficit_ref[:, here],
                state_ref[:, here],
                wide[:, g * sub_block : (g + 1) * sub_block + 2 * MARGIN],
            ],
            axis=1,
        )
        out_ref[g, :half, :] = jnp.concatenate([piece[:half], piece[half:members]], axis=1)


def analysis_kernel(got_ref, across_ref, table_ref, out_ref, all_ref):
    groups_m, _, width = got_ref.shape
    width = width // 2
    ensemble = all_ref.shape[1]
    half = ensemble // groups_m // 2
    sub_block = (width - 2 * MARGIN) // 3
    window = sub_block + 2 * MARGIN
    halves, _, lanes = table_ref.shape
    count = lanes // window
    for g in range(groups_m):
        for side in range(2):
            at = (2 * g + side) * half
            part = slice(side * width, (side + 1) * width)
            all_ref[0, at : at + half, :] = got_ref[g, :half, part]
            all_ref[1, at : at + half, :] = across_ref[g, :half, part]
    values = all_ref[0]
    rates = values[:, 2 * sub_block :]
    beyond = all_ref[1][:, 2 * sub_block :]
    beyond = jnp.concatenate([beyond[:, sub_block:], beyond[:, :sub_block]], axis=1)
    edge = table_ref[0, 2 * window + 2 : 2 * window + 3, :window]
    rates = jnp.where(edge > 0, beyond, rates)
    starts = (0, sub_block, 2 * sub_block + MARGIN)
    pieces = [rates]
    for h in range(halves):
        pieces += [values[:, s + h * count : s + (h + 1) * count] for s in starts]
    turned = jnp.transpose(jnp.concatenate(pieces, axis=1))
    turned_mean = jnp.mean(turned, axis=1, keepdims=True)
    turned = turned - turned_mean
    rates_tiled = jnp.concatenate([rates] * count, axis=1)
    mean_tiled = jnp.mean(rates_tiled, axis=0, keepdims=True)
    y = split(rates_tiled - mean_tiled, 3)
    grams = product(turned, y)
    gram = grams[:window]
    row = lax.broadcasted_iota(jnp.int32, (window, lanes), 0)
    lane = lax.broadcasted_iota(jnp.int32, (window, lanes), 1)
    eye = jnp.where(row == lane % window, 1.0, 0.0).astype(F32)
    block_row = lax.broadcasted_iota(jnp.int32, (lanes, lanes), 0) // window
    block_lane = lax.broadcasted_iota(jnp.int32, (lanes, lanes), 1) // window
    on_block = block_row == block_lane
    diag = jnp.sum(
        jnp.where(
            lax.broadcasted_iota(jnp.int32, (window, window), 0)
            == lax.broadcasted_iota(jnp.int32, (window, window), 1),
            gram[:, :window],
            0.0,
        ),
        axis=1,
        keepdims=True,
    )
    vrows = 3 * count
    own = lax.broadcasted_iota(jnp.int32, (vrows, lanes), 0) % count == (
        lax.broadcasted_iota(jnp.int32, (vrows, lanes), 1) // window
    )
    first = own & (lax.broadcasted_iota(jnp.int32, (vrows, lanes), 1) % window == 0)

    def blocks(x, parts=2):
        return tuple(
            jnp.where(on_block, jnp.concatenate([part] * count, 0), jnp.zeros((), BF16))
            for part in split(x, parts)
        )

    free = ensemble - 1.0
    state = []
    for h in range(halves):
        table = table_ref[h]
        cross = gram * table[:window]
        scale = free + jnp.sum(diag * table[window : 2 * window], axis=0, keepdims=True)
        inv = 1.0 / scale
        base = cross * inv
        root = table[2 * window : 2 * window + 1]
        obs = table[2 * window + 1 : 2 * window + 2]
        q = jnp.where(own, grams[window + h * vrows : window + (h + 1) * vrows] * root, 0.0)
        drive = (obs - mean_tiled) * root
        r = free * inv
        state.append(dict(base=base, inv=inv, root=root, q=q, drive=drive, r=r))
    for s in state:
        base, r = s["base"], s["r"]
        full_r = r * eye + base
        g = 1.5 - 0.5 * r
        gain = g * eye - 0.5 * base
        s["S"] = gain - 0.5 * r * eye
        s["T"] = -0.5 * eye
        s["r"], s["z"] = r * g, g
        s["fz"] = gain
        s["fr"] = product(full_r, blocks(gain, PARTS[0]))
    for it in range(1, NS_ITERS):
        last = it == NS_ITERS - 1
        for s in state:
            rb = blocks(s["fr"], PARTS[1])
            if it == 1:
                zr, tr = product(s["fz"], rb), -0.5 * s["fr"]
            else:
                both = product(jnp.concatenate([s["fz"], s["T"]], 0), rb)
                zr, tr = both[:window], both[window:]
            s["G"] = 1.5 * eye - 0.5 * zr
            s["H"] = -0.5 * (s["z"] * s["S"] + tr)
        for s in state:
            g = 1.5 - 0.5 * s["z"] * s["r"]
            s["T"] = g * s["T"] + product(s["H"], blocks(s["fz"], PARTS[2]))
            rows = [s["fz"]] if last else [s["fz"], s["fr"], s["S"]]
            both = product(jnp.concatenate(rows, 0), blocks(s["G"], PARTS[3]))
            s["fz"] = both[:window]
            if not last:
                s["fr"] = both[window : 2 * window]
                s["S"] = both[2 * window :] + s["r"] * s["H"]
            s["r"], s["z"] = s["r"] * g, s["z"] * g
    for h, s in enumerate(state):
        here = slice(window + h * vrows, window + (h + 1) * vrows)
        u = product(s["q"], blocks(s["T"], PARTS[4])) * (s["root"] * s["inv"])
        rows = jnp.concatenate([s["q"], s["drive"], jnp.zeros((7, lanes), F32)], 0)
        through = product(rows, blocks(s["fz"], PARTS[5]))
        factor = jnp.sqrt(free * s["inv"])
        shift = through[:vrows] * (through[vrows : vrows + 1] * s["inv"])
        shift = jnp.sum(shift, axis=1, keepdims=True)
        keep = jnp.sum(jnp.where(first, s["z"] * factor, 0.0), axis=1, keepdims=True)
        spread = product(u * factor, y, (((1,), (1,)), ((), ())))
        result = turned_mean[here] + shift + keep * turned[here] + spread
        for v in range(3):
            out_ref[v, h * count : (h + 1) * count, :] = result[v * count : (v + 1) * count]


def pack(deficit, state_log, rates, members, count):
    own = rates.shape[1]
    width = 2 * (3 * (own // count) + 2 * MARGIN)
    rows = -(-members // 4) * 2
    return pl.pallas_call(
        functools.partial(pack_kernel, members),
        out_shape=jax.ShapeDtypeStruct((count, rows, width), F32),
        in_specs=[pl.BlockSpec(memory_space=pltpu.VMEM)] * 3,
        out_specs=pl.BlockSpec(memory_space=pltpu.VMEM),
        compiler_params=pltpu.CompilerParams(vmem_limit_bytes=8 * 1024 * 1024),
    )(deficit, state_log, rates)


def analyse(received, across, table, ensemble):
    width = received.shape[2] // 2
    sub_block = (width - 2 * MARGIN) // 3
    return pl.pallas_call(
        analysis_kernel,
        out_shape=jax.ShapeDtypeStruct((3, sub_block, ensemble), F32),
        in_specs=[pl.BlockSpec(memory_space=pltpu.VMEM)] * 3,
        out_specs=pl.BlockSpec(memory_space=pltpu.VMEM),
        scratch_shapes=[pltpu.VMEM((2, ensemble, width), F32)],
        compiler_params=pltpu.CompilerParams(vmem_limit_bytes=16 * 1024 * 1024),
    )(received, across, table)


def in_pieces(x):
    pieces = []
    for _ in range(3):
        pieces.append(lax.reduce_precision(x, exponent_bits=8, mantissa_bits=7))
        x = x - pieces[-1]
    return jnp.stack(pieces).astype(BF16)


def body(
    kernel_rows,
    row_scale,
    self_stiffness,
    base_stress,
    friction_rate,
    damping,
    deficit_start,
    state_start,
    obs_rate,
    obs_precision,
):
    groups = lax.axis_size("member")
    blocks = lax.axis_size("patch")
    own_rows = kernel_rows.shape[0]
    members = deficit_start.shape[0]
    sub_block = own_rows // groups
    pair = 2 if members % 2 == 0 else 1

    def paired(rounded):
        return jnp.stack([rounded[i : i + pair] for i in range(0, members, pair)])

    def joined(blocks):
        return joined_along(blocks.reshape(blocks.shape[0], members, own_rows), 1)

    def gather(rounded):
        return joined(from_everyone(paired(rounded), "patch"))

    def tendency(gathered, deficit, state_log, guess):
        velocity = section_rate(gathered, deficit, state_log, guess)
        return (plate_rate - velocity, jnp.exp(-state_log) - jnp.abs(velocity), velocity)

    def section_rate(gathered, deficit, state_log, guess):
        total = lax.dot_general(
            gathered,
            kernel_rows,
            (((1,), (1,)), ((), ())),
            preferred_element_type=F32,
        )
        stress = base_stress + self_stiffness * deficit + row_scale * total
        return slip_rate(stress, state_log, guess, friction_rate, damping)

    observed = jnp.stack([obs_rate, obs_precision])
    ends = jnp.stack([observed[:, :MARGIN], observed[:, own_rows - MARGIN :]])
    spare = in_pieces(ends).reshape(1, -1)
    spare = jnp.pad(spare, ((0, pair - 1), (0, own_rows - spare.shape[1])))[None]
    deficit = deficit_start
    state_log = state_start
    velocity = jnp.zeros_like(deficit)
    rounded, group_index, block_index = lax.optimization_barrier(
        (
            jnp.concatenate([paired(deficit_start.astype(BF16)), spare], axis=0),
            lax.axis_index("member"),
            lax.axis_index("patch"),
        )
    )
    first = from_everyone(rounded, "patch")
    first, friction_rate, damping, row_scale, self_stiffness, base_stress = lax.optimization_barrier(
        (first, friction_rate, damping, row_scale, self_stiffness, base_stress)
    )
    gathered = joined(first[:, : members // pair])
    for step in range(STEPS):
        deficit_zero, state_zero = (deficit, state_log)
        if step > 0:
            gathered = gather(deficit_zero.astype(BF16))
        change, state_change, velocity = tendency(gathered, deficit_zero, state_zero, velocity)
        deficit_one = deficit_zero + time_step * change
        state_one = state_zero + time_step * state_change
        change, state_change, velocity = tendency(
            gather(deficit_one.astype(BF16)), deficit_one, state_one, velocity
        )
        deficit_two = 0.75 * deficit_zero + 0.25 * (deficit_one + time_step * change)
        state_two = 0.75 * state_zero + 0.25 * (state_one + time_step * state_change)
        change, state_change, velocity = tendency(
            gather(deficit_two.astype(BF16)), deficit_two, state_two, velocity
        )
        deficit = deficit_zero / 3.0 + 2.0 / 3.0 * (deficit_two + time_step * change)
        state_log = state_zero / 3.0 + 2.0 / 3.0 * (state_two + time_step * state_change)
    deficit, state_log, velocity = lax.optimization_barrier((deficit, state_log, velocity))
    forecast = section_rate(gather(deficit.astype(BF16)), deficit, state_log, velocity)
    sent = pack(deficit, state_log, forecast, members, groups)
    received = lax.all_to_all(sent, "member", split_axis=0, concat_axis=0, tiled=True)
    received, first, obs_rate, obs_precision, group_index, block_index = lax.optimization_barrier(
        (received, first, obs_rate, obs_precision, group_index, block_index)
    )
    observed = jnp.stack([obs_rate, obs_precision])
    spare = first[:, members // pair, 0]
    pairs = [((groups - 1) * blocks + p, p + 1) for p in range(blocks - 1)]
    pairs += [(b, a) for a, b in pairs]
    across = lax.ppermute(received, ("member", "patch"), pairs)

    def ends_of(block):
        row = lax.dynamic_index_in_dim(spare, jnp.clip(block, 0, blocks - 1), 0, keepdims=False)
        parts = row[: 3 * ends.size].astype(F32).reshape(3, *ends.shape)
        there = (block >= 0) & (block < blocks)
        return jnp.where(there, parts[0] + (parts[1] + parts[2]), 0.0)

    observed = jnp.concatenate(
        [ends_of(block_index - 1)[1], observed, ends_of(block_index + 1)[0]], axis=1
    )
    obs_window = lax.dynamic_slice_in_dim(
        observed, group_index * sub_block, sub_block + 2 * MARGIN, 1
    )
    table = tables(obs_window, sub_block, group_index, groups)
    analysis = jnp.transpose(analyse(received, across, table, members * groups), (0, 2, 1))
    return analysis[:, :, None, :]


def solution(mesh):
    return jax.shard_map(
        body,
        mesh=mesh,
        in_specs=(
            P("patch", None),
            P("patch"),
            P("patch"),
            P("patch"),
            P("patch"),
            P("patch"),
            P("member", "patch"),
            P("member", "patch"),
            P("patch"),
            P("patch"),
        ),
        out_specs=P(None, None, "patch", "member"),
        check_vma=False,
    )
```

```python
import functools
import jax
import numpy as np
import jax.numpy as jnp
from jax import lax
from jax.experimental import pallas as pl
from jax.experimental.pallas import tpu as pltpu
from jax.sharding import PartitionSpec as P

STEPS = 2
NEWTON = 4
NS_ITERS = 6
MARGIN = 8
F32, BF16 = jnp.float32, jnp.bfloat16
PARTS = (3, 2, 2, 3, 2, 3)
LANES = 128
BESIDE = 2
LN2 = 0.6931471805599453


time_step = 0.25
plate_rate = 1.0

def from_everyone(x, axis):
    copies = jnp.broadcast_to(x, (lax.axis_size(axis), *x.shape))
    return lax.all_to_all(copies, axis, split_axis=0, concat_axis=0, tiled=True)


def joined_along(blocks, dim):
    blocks = jnp.moveaxis(blocks, 0, dim)
    dims = blocks.shape
    return blocks.reshape(*dims[:dim], dims[dim] * dims[dim + 1], *dims[dim + 2 :])


def inverse_sinh(value):
    magnitude = jnp.abs(value)
    result = jnp.log(magnitude + jnp.sqrt(magnitude * magnitude + 1.0))
    return jnp.where(value < 0, -result, result)


def slip_rate(stress, state_log, guess, friction_rate, damping):
    factor = jnp.exp(state_log / friction_rate - LN2)
    velocity = guess
    for _ in range(NEWTON):
        scaled = factor * velocity
        residual = friction_rate * inverse_sinh(scaled) + damping * velocity - stress
        derivative = friction_rate * factor / jnp.sqrt(1.0 + scaled * scaled) + damping
        velocity = velocity - residual / derivative
    return velocity


def split(x, parts=2):
    pieces = []
    for _ in range(parts):
        pieces.append(x.astype(BF16))
        x = x - pieces[-1].astype(F32)
    return pieces


def product(rows, right, dims=(((1,), (0,)), ((), ()))):
    left = split(rows, len(right))
    count = rows.shape[0]
    total = None
    for i, piece in reversed(list(enumerate(right))):
        stacked = jnp.concatenate(left[: len(right) - i], 0)
        sums = lax.dot_general(stacked, piece, dims, preferred_element_type=F32)
        for j in reversed(range(len(right) - i)):
            term = sums[j * count : (j + 1) * count]
            total = term if total is None else total + term
    return total


def tables(obs_window, sub_block, group_index, groups):
    window = sub_block + 2 * MARGIN
    together = LANES // window
    sets = sub_block // together
    distance = np.abs(np.arange(sub_block)[:, None] + MARGIN - np.arange(window)[None, :])
    taper = np.where(distance <= MARGIN, np.exp(-0.5 * (distance / MARGIN) ** 2), 0.0)
    taper = taper.reshape(sets, together, window)
    across = np.broadcast_to(
        np.transpose(taper, (0, 2, 1))[:, :, :, None], (sets, window, together, window)
    ).reshape(sets, window, LANES)
    along = taper.reshape(sets, 1, LANES)
    root = np.sqrt(across * along).astype(np.float32)
    root_along = np.sqrt(along).astype(np.float32)
    across = across.astype(np.float32)
    precision = obs_window[1]
    root_precision = jnp.sqrt(precision)
    root_tiled = jnp.tile(root_precision, together)[None, None, :]
    lane = np.arange(LANES)
    from_across = ((lane == 0) & (group_index == 0)) | ((lane == 1) & (group_index == groups - 1))
    rows = jnp.stack([jnp.tile(obs_window[0], together), from_across.astype(F32)])
    return jnp.concatenate(
        [
            root * root_precision[None, :, None] * root_tiled,
            across * precision[None, :, None],
            root_along * root_tiled,
            jnp.broadcast_to(rows[None], (sets, 2, LANES)),
            jnp.zeros((sets, 5, LANES), F32),
        ],
        axis=1,
    )


def pack_kernel(members, deficit_ref, state_ref, rate_ref, out_ref):
    count, rows, width = out_ref.shape
    own = rate_ref.shape[1]
    sub_block = own // count
    rates = rate_ref[...]
    rim = jnp.zeros((members, MARGIN), F32)
    wide = jnp.concatenate([rim, rates, rim], axis=1)
    used = 3 * sub_block + 4 * MARGIN
    tail = [rates[:, :MARGIN], rates[:, own - MARGIN :], jnp.zeros((members, width - used), F32)]
    out_ref[...] = jnp.zeros(out_ref.shape, F32)
    for g in range(count):
        here = slice(g * sub_block, (g + 1) * sub_block)
        window = wide[:, g * sub_block : (g + 1) * sub_block + 2 * MARGIN]
        out_ref[g, :members, :] = jnp.concatenate(
            [deficit_ref[:, here], state_ref[:, here], window, *tail], axis=1
        )


def turn_kernel(members, got_ref, turned_ref, ends_ref, all_ref):
    for g in range(got_ref.shape[0]):
        all_ref[g * members : (g + 1) * members, :] = got_ref[g, :members, :]
    ensemble = all_ref.shape[0]
    turned = jnp.transpose(all_ref[...])
    sub_block = (turned_ref.shape[0] - 2 * MARGIN) // 4
    window = sub_block + 2 * MARGIN
    together = LANES // window
    start = 2 * sub_block
    turned_ref[:window, :] = turned[start : start + window]
    for h in range(sub_block // together):
        for v, s in enumerate((0, sub_block, start + MARGIN)):
            at = window + (3 * h + v) * together
            turned_ref[at : at + together, :] = turned[s + h * together : s + (h + 1) * together]
    ends_ref[...] = jnp.zeros(ends_ref.shape, F32)
    ends_ref[:, :ensemble] = turned[start + window : start + window + 2 * MARGIN]


def analysis_kernel(turned_ref, across_ref, table_ref, out_ref):
    ensemble = turned_ref.shape[1]
    halves, _, lanes = table_ref.shape
    window = (table_ref.shape[1] - 8) // 2
    sub_block = window - 2 * MARGIN
    count = lanes // window
    flags = table_ref[0, 2 * window + 2 : 2 * window + 3, :]
    turned = turned_ref[...]
    turned = jnp.concatenate(
        [
            jnp.where(flags[:, 0:1] > 0, across_ref[MARGIN:, :ensemble], turned[:MARGIN]),
            turned[MARGIN : window - MARGIN],
            jnp.where(flags[:, 1:2] > 0, across_ref[:MARGIN, :ensemble], turned[window - MARGIN : window]),
            turned[window:],
        ],
        axis=0,
    )
    rates = jnp.transpose(turned[:window])
    turned_mean = jnp.mean(turned, axis=1, keepdims=True)
    turned = turned - turned_mean
    rates_tiled = jnp.concatenate([rates] * count, axis=1)
    mean_tiled = jnp.mean(rates_tiled, axis=0, keepdims=True)
    y = split(rates_tiled - mean_tiled, 3)
    grams = product(turned, y)
    gram = grams[:window]
    row = lax.broadcasted_iota(jnp.int32, (window, lanes), 0)
    lane = lax.broadcasted_iota(jnp.int32, (window, lanes), 1)
    eye = jnp.where(row == lane % window, 1.0, 0.0).astype(F32)
    block_row = lax.broadcasted_iota(jnp.int32, (lanes, lanes), 0) // window
    block_lane = lax.broadcasted_iota(jnp.int32, (lanes, lanes), 1) // window
    on_block = block_row == block_lane
    diag = jnp.sum(
        jnp.where(
            lax.broadcasted_iota(jnp.int32, (window, window), 0)
            == lax.broadcasted_iota(jnp.int32, (window, window), 1),
            gram[:, :window],
            0.0,
        ),
        axis=1,
        keepdims=True,
    )
    vrows = 3 * count
    own = lax.broadcasted_iota(jnp.int32, (vrows, lanes), 0) % count == (
        lax.broadcasted_iota(jnp.int32, (vrows, lanes), 1) // window
    )
    first = own & (lax.broadcasted_iota(jnp.int32, (vrows, lanes), 1) % window == 0)

    def blocks(x, parts=2):
        return tuple(
            jnp.where(on_block, jnp.concatenate([part] * count, 0), jnp.zeros((), BF16))
            for part in split(x, parts)
        )

    free = ensemble - 1.0
    state = []
    for h in range(halves):
        table = table_ref[h]
        cross = gram * table[:window]
        scale = free + jnp.sum(diag * table[window : 2 * window], axis=0, keepdims=True)
        inv = 1.0 / scale
        base = cross * inv
        root = table[2 * window : 2 * window + 1]
        obs = table[2 * window + 1 : 2 * window + 2]
        q = jnp.where(own, grams[window + h * vrows : window + (h + 1) * vrows] * root, 0.0)
        drive = (obs - mean_tiled) * root
        r = free * inv
        state.append(dict(base=base, inv=inv, root=root, q=q, drive=drive, r=r))
    for s in state:
        base, r = s["base"], s["r"]
        full_r = r * eye + base
        g = 1.5 - 0.5 * r
        gain = g * eye - 0.5 * base
        s["S"] = gain - 0.5 * r * eye
        s["T"] = -0.5 * eye
        s["r"], s["z"] = r * g, g
        s["fz"] = gain
        s["fr"] = product(full_r, blocks(gain, PARTS[0]))
    for it in range(1, NS_ITERS):
        last = it == NS_ITERS - 1
        for s in state:
            rb = blocks(s["fr"], PARTS[1])
            if it == 1:
                zr, tr = product(s["fz"], rb), -0.5 * s["fr"]
            else:
                both = product(jnp.concatenate([s["fz"], s["T"]], 0), rb)
                zr, tr = both[:window], both[window:]
            s["G"] = 1.5 * eye - 0.5 * zr
            s["H"] = -0.5 * (s["z"] * s["S"] + tr)
        for s in state:
            g = 1.5 - 0.5 * s["z"] * s["r"]
            s["T"] = g * s["T"] + product(s["H"], blocks(s["fz"], PARTS[2]))
            rows = [s["fz"]] if last else [s["fz"], s["fr"], s["S"]]
            both = product(jnp.concatenate(rows, 0), blocks(s["G"], PARTS[3]))
            s["fz"] = both[:window]
            if not last:
                s["fr"] = both[window : 2 * window]
                s["S"] = both[2 * window :] + s["r"] * s["H"]
            s["r"], s["z"] = s["r"] * g, s["z"] * g
    for h, s in enumerate(state):
        here = slice(window + h * vrows, window + (h + 1) * vrows)
        u = product(s["q"], blocks(s["T"], PARTS[4])) * (s["root"] * s["inv"])
        rows = jnp.concatenate([s["q"], s["drive"], jnp.zeros((7, lanes), F32)], 0)
        through = product(rows, blocks(s["fz"], PARTS[5]))
        factor = jnp.sqrt(free * s["inv"])
        shift = through[:vrows] * (through[vrows : vrows + 1] * s["inv"])
        shift = jnp.sum(shift, axis=1, keepdims=True)
        keep = jnp.sum(jnp.where(first, s["z"] * factor, 0.0), axis=1, keepdims=True)
        spread = product(u * factor, y, (((1,), (1,)), ((), ())))
        result = turned_mean[here] + shift + keep * turned[here] + spread
        for v in range(3):
            out_ref[v, h * count : (h + 1) * count, :] = result[v * count : (v + 1) * count]


def pack(deficit, state_log, rates, count):
    members = rates.shape[0]
    return pl.pallas_call(
        functools.partial(pack_kernel, members),
        out_shape=jax.ShapeDtypeStruct((count, -(-members // 8) * 8, LANES), F32),
        in_specs=[pl.BlockSpec(memory_space=pltpu.VMEM)] * 3,
        out_specs=pl.BlockSpec(memory_space=pltpu.VMEM),
        compiler_params=pltpu.CompilerParams(vmem_limit_bytes=8 * 1024 * 1024),
    )(deficit, state_log, rates)


def turn(received, members, sub_block):
    ensemble = received.shape[0] * members
    return pl.pallas_call(
        functools.partial(turn_kernel, members),
        out_shape=(
            jax.ShapeDtypeStruct((4 * sub_block + 2 * MARGIN, ensemble), F32),
            jax.ShapeDtypeStruct((2 * MARGIN, -(-ensemble // 128) * 128), F32),
        ),
        in_specs=[pl.BlockSpec(memory_space=pltpu.VMEM)],
        out_specs=(pl.BlockSpec(memory_space=pltpu.VMEM),) * 2,
        scratch_shapes=[pltpu.VMEM((ensemble, received.shape[2]), F32)],
        compiler_params=pltpu.CompilerParams(vmem_limit_bytes=8 * 1024 * 1024),
    )(received)


def analyse(turned, across, table):
    sub_block = (turned.shape[0] - 2 * MARGIN) // 4
    return pl.pallas_call(
        analysis_kernel,
        out_shape=jax.ShapeDtypeStruct((3, sub_block, turned.shape[1]), F32),
        in_specs=[pl.BlockSpec(memory_space=pltpu.VMEM)] * 3,
        out_specs=pl.BlockSpec(memory_space=pltpu.VMEM),
        compiler_params=pltpu.CompilerParams(vmem_limit_bytes=16 * 1024 * 1024),
    )(turned, across, table)


def in_pieces(x):
    pieces = []
    for _ in range(3):
        pieces.append(lax.reduce_precision(x, exponent_bits=8, mantissa_bits=7))
        x = x - pieces[-1]
    return jnp.stack(pieces).astype(BF16)


def body(
    kernel_rows,
    row_scale,
    self_stiffness,
    base_stress,
    friction_rate,
    damping,
    deficit_start,
    state_start,
    obs_rate,
    obs_precision,
):
    groups = lax.axis_size("member")
    blocks = lax.axis_size("patch")
    own_rows = kernel_rows.shape[0]
    members = deficit_start.shape[0]
    sub_block = own_rows // groups
    pair = 2 if members % 2 == 0 else 1

    def paired(rounded):
        return jnp.stack([rounded[i : i + pair] for i in range(0, members, pair)])

    def joined(blocks):
        return joined_along(blocks.reshape(blocks.shape[0], members, own_rows), 1)

    def gather(rounded):
        return joined(from_everyone(paired(rounded), "patch"))

    def tendency(gathered, deficit, state_log, guess):
        velocity = section_rate(gathered, deficit, state_log, guess)
        return (plate_rate - velocity, jnp.exp(-state_log) - jnp.abs(velocity), velocity)

    def section_rate(gathered, deficit, state_log, guess):
        total = lax.dot_general(
            gathered,
            kernel_rows,
            (((1,), (1,)), ((), ())),
            preferred_element_type=F32,
        )
        stress = base_stress + self_stiffness * deficit + row_scale * total
        return slip_rate(stress, state_log, guess, friction_rate, damping)

    observed = jnp.stack([obs_rate, obs_precision])
    ends = jnp.stack([observed[:, :MARGIN], observed[:, own_rows - MARGIN :]])
    spare = in_pieces(ends).reshape(1, -1)
    spare = jnp.pad(spare, ((0, pair - 1), (0, own_rows - spare.shape[1])))[None]
    deficit = deficit_start
    state_log = state_start
    rounded, velocity, group_index, block_index = lax.optimization_barrier(
        (
            jnp.concatenate([paired(deficit_start.astype(BF16)), spare], axis=0),
            jnp.zeros_like(deficit),
            lax.axis_index("member"),
            lax.axis_index("patch"),
        )
    )
    first = from_everyone(rounded, "patch")
    first, friction_rate, damping, row_scale, self_stiffness, base_stress = lax.optimization_barrier(
        (first, friction_rate, damping, row_scale, self_stiffness, base_stress)
    )
    gathered = joined(first[:, : members // pair])
    for step in range(STEPS):
        deficit_zero, state_zero = (deficit, state_log)
        if step > 0:
            gathered = gather(deficit_zero.astype(BF16))
        change, state_change, velocity = tendency(gathered, deficit_zero, state_zero, velocity)
        deficit_one = deficit_zero + time_step * change
        state_one = state_zero + time_step * state_change
        change, state_change, velocity = tendency(
            gather(deficit_one.astype(BF16)), deficit_one, state_one, velocity
        )
        deficit_two = 0.75 * deficit_zero + 0.25 * (deficit_one + time_step * change)
        state_two = 0.75 * state_zero + 0.25 * (state_one + time_step * state_change)
        change, state_change, velocity = tendency(
            gather(deficit_two.astype(BF16)), deficit_two, state_two, velocity
        )
        deficit = deficit_zero / 3.0 + 2.0 / 3.0 * (deficit_two + time_step * change)
        state_log = state_zero / 3.0 + 2.0 / 3.0 * (state_two + time_step * state_change)
    deficit, state_log, velocity = lax.optimization_barrier((deficit, state_log, velocity))
    forecast = section_rate(gather(deficit.astype(BF16)), deficit, state_log, velocity)
    sent = pack(deficit, state_log, forecast, groups)
    received = lax.all_to_all(sent, "member", split_axis=0, concat_axis=0, tiled=True)
    turned, own_ends = turn(received, members, sub_block)
    turned, own_ends, first, obs_rate, obs_precision, group_index, block_index = (
        lax.optimization_barrier(
            (turned, own_ends, first, obs_rate, obs_precision, group_index, block_index)
        )
    )
    observed = jnp.stack([obs_rate, obs_precision])
    spare = first[:, members // pair, 0]
    last = groups - 1
    pairs = [(BESIDE * blocks + p, p + 1) for p in range(blocks - 1)]
    pairs += [((last - BESIDE) * blocks + p + 1, last * blocks + p) for p in range(blocks - 1)]
    across = lax.ppermute(own_ends, ("member", "patch"), pairs)

    def ends_of(block):
        row = lax.dynamic_index_in_dim(spare, jnp.clip(block, 0, blocks - 1), 0, keepdims=False)
        parts = row[: 3 * ends.size].astype(F32).reshape(3, *ends.shape)
        there = (block >= 0) & (block < blocks)
        return jnp.where(there, parts[0] + (parts[1] + parts[2]), 0.0)

    observed = jnp.concatenate(
        [ends_of(block_index - 1)[1], observed, ends_of(block_index + 1)[0]], axis=1
    )
    obs_window = lax.dynamic_slice_in_dim(
        observed, group_index * sub_block, sub_block + 2 * MARGIN, 1
    )
    table = tables(obs_window, sub_block, group_index, groups)
    analysis = jnp.transpose(analyse(turned, across, table), (0, 2, 1))
    return analysis[:, :, None, :]


def solution(mesh):
    return jax.shard_map(
        body,
        mesh=mesh,
        in_specs=(
            P("patch", None),
            P("patch"),
            P("patch"),
            P("patch"),
            P("patch"),
            P("patch"),
            P("member", "patch"),
            P("member", "patch"),
            P("patch"),
            P("patch"),
        ),
        out_specs=P(None, None, "patch", "member"),
        check_vma=False,
    )
```

```python
import functools
import jax
import numpy as np
import jax.numpy as jnp
from jax import lax
from jax.experimental import pallas as pl
from jax.experimental.pallas import tpu as pltpu
from jax.sharding import PartitionSpec as P

STEPS = 2
NEWTON = 4
NS_ITERS = 6
MARGIN = 8
F32, BF16 = jnp.float32, jnp.bfloat16
PARTS = (3, 2, 2, 3, 2, 3)
LANES = 128
BESIDE = 2
LN2 = 0.6931471805599453


time_step = 0.25
plate_rate = 1.0

def from_everyone(x, axis):
    copies = jnp.broadcast_to(x, (lax.axis_size(axis), *x.shape))
    return lax.all_to_all(copies, axis, split_axis=0, concat_axis=0, tiled=True)


def joined_along(blocks, dim):
    blocks = jnp.moveaxis(blocks, 0, dim)
    dims = blocks.shape
    return blocks.reshape(*dims[:dim], dims[dim] * dims[dim + 1], *dims[dim + 2 :])


def slip_rate(stress, state_log, guess, friction_rate, damping):
    factor = jnp.exp(state_log / friction_rate - LN2)
    slope = friction_rate * factor
    velocity = guess
    for _ in range(NEWTON):
        scaled = factor * velocity
        magnitude = jnp.abs(scaled)
        root = jnp.sqrt(scaled * scaled + 1.0)
        angle = jnp.log(magnitude + root)
        angle = jnp.where(scaled < 0, -angle, angle)
        residual = friction_rate * angle + damping * velocity - stress
        velocity = velocity - residual * root / (slope + damping * root)
    return velocity


def split(x, parts=2):
    pieces = []
    for _ in range(parts):
        pieces.append(x.astype(BF16))
        x = x - pieces[-1].astype(F32)
    return pieces


def product(rows, right, dims=(((1,), (0,)), ((), ()))):
    left = split(rows, len(right))
    count = rows.shape[0]
    total = None
    for i, piece in reversed(list(enumerate(right))):
        stacked = jnp.concatenate(left[: len(right) - i], 0)
        sums = lax.dot_general(stacked, piece, dims, preferred_element_type=F32)
        for j in reversed(range(len(right) - i)):
            term = sums[j * count : (j + 1) * count]
            total = term if total is None else total + term
    return total


def tables(obs_window, sub_block, group_index, groups):
    window = sub_block + 2 * MARGIN
    together = LANES // window
    sets = sub_block // together
    distance = np.abs(np.arange(sub_block)[:, None] + MARGIN - np.arange(window)[None, :])
    taper = np.where(distance <= MARGIN, np.exp(-0.5 * (distance / MARGIN) ** 2), 0.0)
    taper = taper.reshape(sets, together, window)
    across = np.broadcast_to(
        np.transpose(taper, (0, 2, 1))[:, :, :, None], (sets, window, together, window)
    ).reshape(sets, window, LANES)
    along = taper.reshape(sets, 1, LANES)
    root = np.sqrt(across * along).astype(np.float32)
    root_along = np.sqrt(along).astype(np.float32)
    across = across.astype(np.float32)
    precision = obs_window[1]
    root_precision = jnp.sqrt(precision)
    root_tiled = jnp.tile(root_precision, together)[None, None, :]
    lane = np.arange(LANES)
    from_across = ((lane == 0) & (group_index == 0)) | ((lane == 1) & (group_index == groups - 1))
    rows = jnp.stack([jnp.tile(obs_window[0], together), from_across.astype(F32)])
    return jnp.concatenate(
        [
            root * root_precision[None, :, None] * root_tiled,
            across * precision[None, :, None],
            root_along * root_tiled,
            jnp.broadcast_to(rows[None], (sets, 2, LANES)),
            jnp.zeros((sets, 5, LANES), F32),
        ],
        axis=1,
    )


def pack_kernel(members, deficit_ref, state_ref, rate_ref, out_ref):
    count, rows, width = out_ref.shape
    own = rate_ref.shape[1]
    sub_block = own // count
    rates = rate_ref[...]
    rim = jnp.zeros((members, MARGIN), F32)
    wide = jnp.concatenate([rim, rates, rim], axis=1)
    used = 3 * sub_block + 4 * MARGIN
    tail = [rates[:, :MARGIN], rates[:, own - MARGIN :], jnp.zeros((members, width - used), F32)]
    out_ref[...] = jnp.zeros(out_ref.shape, F32)
    for g in range(count):
        here = slice(g * sub_block, (g + 1) * sub_block)
        window = wide[:, g * sub_block : (g + 1) * sub_block + 2 * MARGIN]
        out_ref[g, :members, :] = jnp.concatenate(
            [deficit_ref[:, here], state_ref[:, here], window, *tail], axis=1
        )


def turn_kernel(members, got_ref, turned_ref, ends_ref, all_ref):
    for g in range(got_ref.shape[0]):
        all_ref[g * members : (g + 1) * members, :] = got_ref[g, :members, :]
    ensemble = all_ref.shape[0]
    turned = jnp.transpose(all_ref[...])
    sub_block = (turned_ref.shape[0] - 2 * MARGIN) // 4
    window = sub_block + 2 * MARGIN
    together = LANES // window
    start = 2 * sub_block
    turned_ref[:window, :] = turned[start : start + window]
    for h in range(sub_block // together):
        for v, s in enumerate((0, sub_block, start + MARGIN)):
            at = window + (3 * h + v) * together
            turned_ref[at : at + together, :] = turned[s + h * together : s + (h + 1) * together]
    ends_ref[...] = jnp.zeros(ends_ref.shape, F32)
    ends_ref[:, :ensemble] = turned[start + window : start + window + 2 * MARGIN]


def analysis_kernel(turned_ref, across_ref, table_ref, out_ref):
    ensemble = turned_ref.shape[1]
    halves, _, lanes = table_ref.shape
    window = (table_ref.shape[1] - 8) // 2
    sub_block = window - 2 * MARGIN
    count = lanes // window
    flags = table_ref[0, 2 * window + 2 : 2 * window + 3, :]
    turned = turned_ref[...]
    turned = jnp.concatenate(
        [
            jnp.where(flags[:, 0:1] > 0, across_ref[MARGIN:, :ensemble], turned[:MARGIN]),
            turned[MARGIN : window - MARGIN],
            jnp.where(flags[:, 1:2] > 0, across_ref[:MARGIN, :ensemble], turned[window - MARGIN : window]),
            turned[window:],
        ],
        axis=0,
    )
    rates = jnp.transpose(turned[:window])
    turned_mean = jnp.mean(turned, axis=1, keepdims=True)
    turned = turned - turned_mean
    rates_tiled = jnp.concatenate([rates] * count, axis=1)
    mean_tiled = jnp.mean(rates_tiled, axis=0, keepdims=True)
    y = split(rates_tiled - mean_tiled, 3)
    grams = product(turned, y)
    gram = grams[:window]
    row = lax.broadcasted_iota(jnp.int32, (window, lanes), 0)
    lane = lax.broadcasted_iota(jnp.int32, (window, lanes), 1)
    eye = jnp.where(row == lane % window, 1.0, 0.0).astype(F32)
    block_row = lax.broadcasted_iota(jnp.int32, (lanes, lanes), 0) // window
    block_lane = lax.broadcasted_iota(jnp.int32, (lanes, lanes), 1) // window
    on_block = block_row == block_lane
    diag = jnp.sum(
        jnp.where(
            lax.broadcasted_iota(jnp.int32, (window, window), 0)
            == lax.broadcasted_iota(jnp.int32, (window, window), 1),
            gram[:, :window],
            0.0,
        ),
        axis=1,
        keepdims=True,
    )
    vrows = 3 * count
    own = lax.broadcasted_iota(jnp.int32, (vrows, lanes), 0) % count == (
        lax.broadcasted_iota(jnp.int32, (vrows, lanes), 1) // window
    )
    first = own & (lax.broadcasted_iota(jnp.int32, (vrows, lanes), 1) % window == 0)

    def blocks(x, parts=2):
        return tuple(
            jnp.where(on_block, jnp.concatenate([part] * count, 0), jnp.zeros((), BF16))
            for part in split(x, parts)
        )

    free = ensemble - 1.0
    state = []
    for h in range(halves):
        table = table_ref[h]
        cross = gram * table[:window]
        scale = free + jnp.sum(diag * table[window : 2 * window], axis=0, keepdims=True)
        inv = 1.0 / scale
        base = cross * inv
        root = table[2 * window : 2 * window + 1]
        obs = table[2 * window + 1 : 2 * window + 2]
        q = jnp.where(own, grams[window + h * vrows : window + (h + 1) * vrows] * root, 0.0)
        drive = (obs - mean_tiled) * root
        r = free * inv
        state.append(dict(base=base, inv=inv, root=root, q=q, drive=drive, r=r))
    for s in state:
        base, r = s["base"], s["r"]
        full_r = r * eye + base
        g = 1.5 - 0.5 * r
        gain = g * eye - 0.5 * base
        s["S"] = gain - 0.5 * r * eye
        s["T"] = -0.5 * eye
        s["r"], s["z"] = r * g, g
        s["fz"] = gain
        s["fr"] = product(full_r, blocks(gain, PARTS[0]))
    for it in range(1, NS_ITERS):
        last = it == NS_ITERS - 1
        for s in state:
            rb = blocks(s["fr"], PARTS[1])
            if it == 1:
                zr, tr = product(s["fz"], rb), -0.5 * s["fr"]
            else:
                both = product(jnp.concatenate([s["fz"], s["T"]], 0), rb)
                zr, tr = both[:window], both[window:]
            s["G"] = 1.5 * eye - 0.5 * zr
            s["H"] = -0.5 * (s["z"] * s["S"] + tr)
        for s in state:
            g = 1.5 - 0.5 * s["z"] * s["r"]
            s["T"] = g * s["T"] + product(s["H"], blocks(s["fz"], PARTS[2]))
            rows = [s["fz"]] if last else [s["fz"], s["fr"], s["S"]]
            both = product(jnp.concatenate(rows, 0), blocks(s["G"], PARTS[3]))
            s["fz"] = both[:window]
            if not last:
                s["fr"] = both[window : 2 * window]
                s["S"] = both[2 * window :] + s["r"] * s["H"]
            s["r"], s["z"] = s["r"] * g, s["z"] * g
    for h, s in enumerate(state):
        here = slice(window + h * vrows, window + (h + 1) * vrows)
        u = product(s["q"], blocks(s["T"], PARTS[4])) * (s["root"] * s["inv"])
        rows = jnp.concatenate([s["q"], s["drive"], jnp.zeros((7, lanes), F32)], 0)
        through = product(rows, blocks(s["fz"], PARTS[5]))
        factor = jnp.sqrt(free * s["inv"])
        shift = through[:vrows] * (through[vrows : vrows + 1] * s["inv"])
        shift = jnp.sum(shift, axis=1, keepdims=True)
        keep = jnp.sum(jnp.where(first, s["z"] * factor, 0.0), axis=1, keepdims=True)
        spread = product(u * factor, y, (((1,), (1,)), ((), ())))
        result = turned_mean[here] + shift + keep * turned[here] + spread
        for v in range(3):
            out_ref[v, h * count : (h + 1) * count, :] = result[v * count : (v + 1) * count]


def pack(deficit, state_log, rates, count):
    members = rates.shape[0]
    return pl.pallas_call(
        functools.partial(pack_kernel, members),
        out_shape=jax.ShapeDtypeStruct((count, -(-members // 8) * 8, LANES), F32),
        in_specs=[pl.BlockSpec(memory_space=pltpu.VMEM)] * 3,
        out_specs=pl.BlockSpec(memory_space=pltpu.VMEM),
        compiler_params=pltpu.CompilerParams(vmem_limit_bytes=8 * 1024 * 1024),
    )(deficit, state_log, rates)


def turn(received, members, sub_block):
    ensemble = received.shape[0] * members
    return pl.pallas_call(
        functools.partial(turn_kernel, members),
        out_shape=(
            jax.ShapeDtypeStruct((4 * sub_block + 2 * MARGIN, ensemble), F32),
            jax.ShapeDtypeStruct((2 * MARGIN, -(-ensemble // 128) * 128), F32),
        ),
        in_specs=[pl.BlockSpec(memory_space=pltpu.VMEM)],
        out_specs=(pl.BlockSpec(memory_space=pltpu.VMEM),) * 2,
        scratch_shapes=[pltpu.VMEM((ensemble, received.shape[2]), F32)],
        compiler_params=pltpu.CompilerParams(vmem_limit_bytes=8 * 1024 * 1024),
    )(received)


def analyse(turned, across, table):
    sub_block = (turned.shape[0] - 2 * MARGIN) // 4
    return pl.pallas_call(
        analysis_kernel,
        out_shape=jax.ShapeDtypeStruct((3, sub_block, turned.shape[1]), F32),
        in_specs=[pl.BlockSpec(memory_space=pltpu.VMEM)] * 3,
        out_specs=pl.BlockSpec(memory_space=pltpu.VMEM),
        compiler_params=pltpu.CompilerParams(vmem_limit_bytes=16 * 1024 * 1024),
    )(turned, across, table)


def in_pieces(x):
    pieces = []
    for _ in range(3):
        pieces.append(lax.reduce_precision(x, exponent_bits=8, mantissa_bits=7))
        x = x - pieces[-1]
    return [piece.astype(BF16) for piece in pieces]


def body(
    kernel_rows,
    row_scale,
    self_stiffness,
    base_stress,
    friction_rate,
    damping,
    deficit_start,
    state_start,
    obs_rate,
    obs_precision,
):
    groups = lax.axis_size("member")
    blocks = lax.axis_size("patch")
    own_rows = kernel_rows.shape[0]
    members = deficit_start.shape[0]
    sub_block = own_rows // groups
    pair = 2 if members % 2 == 0 else 1

    def paired(rounded):
        return jnp.stack([rounded[i : i + pair] for i in range(0, members, pair)])

    def joined(blocks):
        return joined_along(blocks.reshape(blocks.shape[0], members, own_rows), 1)

    def gather(rounded):
        return joined(from_everyone(paired(rounded), "patch"))

    def spare_rows(rate, precision):
        ends = [x[at : at + MARGIN] for x in (rate, precision) for at in (0, own_rows - MARGIN)]
        pieces = in_pieces(jnp.concatenate(ends))
        row = jnp.concatenate([*pieces, jnp.zeros((own_rows - 12 * MARGIN,), BF16)])
        return jnp.pad(row[None], ((0, pair - 1), (0, 0)))[None]

    def tendency(gathered, deficit, state_log, guess):
        velocity = section_rate(gathered, deficit, state_log, guess)
        return (plate_rate - velocity, jnp.exp(-state_log) - jnp.abs(velocity), velocity)

    def section_rate(gathered, deficit, state_log, guess):
        total = lax.dot_general(
            gathered,
            kernel_rows,
            (((1,), (1,)), ((), ())),
            preferred_element_type=F32,
        )
        stress = base_stress + self_stiffness * deficit + row_scale * total
        return slip_rate(stress, state_log, guess, friction_rate, damping)

    deficit = deficit_start
    state_log = state_start
    rounded, velocity, group_index, block_index = lax.optimization_barrier(
        (
            paired(deficit_start.astype(BF16)),
            jnp.zeros_like(deficit),
            lax.axis_index("member"),
            lax.axis_index("patch"),
        )
    )
    gathered = from_everyone(rounded, "patch")
    (
        gathered,
        friction_rate,
        damping,
        row_scale,
        self_stiffness,
        base_stress,
    ) = lax.optimization_barrier(
        (gathered, friction_rate, damping, row_scale, self_stiffness, base_stress)
    )
    gathered = joined(gathered)
    for step in range(STEPS):
        deficit_zero, state_zero = (deficit, state_log)
        if step > 0:
            gathered = gather(deficit_zero.astype(BF16))
        change, state_change, velocity = tendency(gathered, deficit_zero, state_zero, velocity)
        deficit_one = deficit_zero + time_step * change
        state_one = state_zero + time_step * state_change
        gathered = gather(deficit_one.astype(BF16))
        if step == 0:
            gathered, obs_rate, obs_precision = lax.optimization_barrier(
                (gathered, obs_rate, obs_precision)
            )
            spare = spare_rows(obs_rate, obs_precision)
        change, state_change, velocity = tendency(gathered, deficit_one, state_one, velocity)
        deficit_two = 0.75 * deficit_zero + 0.25 * (deficit_one + time_step * change)
        state_two = 0.75 * state_zero + 0.25 * (state_one + time_step * state_change)
        rounded = paired(deficit_two.astype(BF16))
        if step == 0:
            third = from_everyone(jnp.concatenate([rounded, spare], axis=0), "patch")
            gathered = joined(third[:, : members // pair])
        else:
            gathered = joined(from_everyone(rounded, "patch"))
        change, state_change, velocity = tendency(gathered, deficit_two, state_two, velocity)
        deficit = deficit_zero / 3.0 + 2.0 / 3.0 * (deficit_two + time_step * change)
        state_log = state_zero / 3.0 + 2.0 / 3.0 * (state_two + time_step * state_change)
    deficit, state_log, velocity = lax.optimization_barrier((deficit, state_log, velocity))
    forecast = section_rate(gather(deficit.astype(BF16)), deficit, state_log, velocity)
    sent = pack(deficit, state_log, forecast, groups)
    received = lax.all_to_all(sent, "member", split_axis=0, concat_axis=0, tiled=True)
    turned, own_ends = turn(received, members, sub_block)
    turned, own_ends, third, obs_rate, obs_precision, group_index, block_index = (
        lax.optimization_barrier(
            (turned, own_ends, third, obs_rate, obs_precision, group_index, block_index)
        )
    )
    last = groups - 1
    pairs = [(BESIDE * blocks + p, p + 1) for p in range(blocks - 1)]
    pairs += [((last - BESIDE) * blocks + p + 1, last * blocks + p) for p in range(blocks - 1)]
    across = lax.ppermute(own_ends, ("member", "patch"), pairs)

    spare = third[:, members // pair, 0].astype(F32)

    def ends_of(block):
        its = np.arange(blocks, dtype=np.int32)[:, None] == block
        row = jnp.sum(jnp.where(its, spare, 0.0), axis=0)
        parts = [row[i * 4 * MARGIN : (i + 1) * 4 * MARGIN] for i in range(3)]
        return parts[0] + (parts[1] + parts[2])

    before, after = ends_of(block_index - 1), ends_of(block_index + 1)

    def window_of(own, at):
        padded = jnp.concatenate(
            [before[at + MARGIN : at + 2 * MARGIN], own, after[at : at + MARGIN]]
        )
        return lax.dynamic_slice_in_dim(padded, group_index * sub_block, sub_block + 2 * MARGIN)

    obs_window = (window_of(obs_rate, 0), window_of(obs_precision, 2 * MARGIN))
    table = tables(obs_window, sub_block, group_index, groups)
    analysis = jnp.transpose(analyse(turned, across, table), (0, 2, 1))
    return analysis[:, :, None, :]


def solution(mesh):
    return jax.shard_map(
        body,
        mesh=mesh,
        in_specs=(
            P("patch", None),
            P("patch"),
            P("patch"),
            P("patch"),
            P("patch"),
            P("patch"),
            P("member", "patch"),
            P("member", "patch"),
            P("patch"),
            P("patch"),
        ),
        out_specs=P(None, None, "patch", "member"),
        check_vma=False,
    )
```

```python
import functools
import jax
import numpy as np
import jax.numpy as jnp
from jax import lax
from jax.experimental import pallas as pl
from jax.experimental.pallas import tpu as pltpu
from jax.sharding import PartitionSpec as P

STEPS = 2
NEWTON = 4
NS_ITERS = 6
MARGIN = 8
F32, BF16 = jnp.float32, jnp.bfloat16
PARTS = (3, 2, 2, 3, 2, 3)
LANES = 128
BESIDE = 2
LN2 = 0.6931471805599453


time_step = 0.25
plate_rate = 1.0

def from_everyone(x, axis):
    copies = jnp.broadcast_to(x, (lax.axis_size(axis), *x.shape))
    return lax.all_to_all(copies, axis, split_axis=0, concat_axis=0, tiled=True)


def joined_along(blocks, dim):
    blocks = jnp.moveaxis(blocks, 0, dim)
    dims = blocks.shape
    return blocks.reshape(*dims[:dim], dims[dim] * dims[dim + 1], *dims[dim + 2 :])


def slip_rate(stress, state_log, guess, friction_rate, damping):
    factor = jnp.exp(state_log / friction_rate - LN2)
    slope = friction_rate * factor
    velocity = guess
    for _ in range(NEWTON):
        scaled = factor * velocity
        magnitude = jnp.abs(scaled)
        root = jnp.sqrt(scaled * scaled + 1.0)
        angle = jnp.log(magnitude + root)
        angle = jnp.where(scaled < 0, -angle, angle)
        residual = friction_rate * angle + damping * velocity - stress
        velocity = velocity - residual * root / (slope + damping * root)
    return velocity


def split(x, parts=2):
    pieces = []
    for _ in range(parts):
        pieces.append(x.astype(BF16))
        x = x - pieces[-1].astype(F32)
    return pieces


def product(rows, right, dims=(((1,), (0,)), ((), ()))):
    left = split(rows, len(right))
    count = rows.shape[0]
    total = None
    for i, piece in reversed(list(enumerate(right))):
        stacked = jnp.concatenate(left[: len(right) - i], 0)
        sums = lax.dot_general(stacked, piece, dims, preferred_element_type=F32)
        for j in reversed(range(len(right) - i)):
            term = sums[j * count : (j + 1) * count]
            total = term if total is None else total + term
    return total


def tapers(sub_block):
    window = sub_block + 2 * MARGIN
    together = LANES // window
    sets = sub_block // together
    distance = np.abs(np.arange(sub_block)[:, None] + MARGIN - np.arange(window)[None, :])
    taper = np.where(distance <= MARGIN, np.exp(-0.5 * (distance / MARGIN) ** 2), 0.0)
    taper = taper.reshape(sets, together, window)
    across = np.broadcast_to(
        np.transpose(taper, (0, 2, 1))[:, :, :, None], (sets, window, together, window)
    ).reshape(sets, window, LANES)
    along = taper.reshape(sets, 1, LANES)
    filler = np.zeros((sets, 7, LANES))
    parts = [np.sqrt(across * along), across, np.sqrt(along), filler]
    return np.concatenate(parts, axis=1).astype(np.float32)


def pack_kernel(deficit_ref, state_ref, rate_ref, obs_ref, precision_ref, out_ref):
    count, rows, width = out_ref.shape
    own = rate_ref.shape[1]
    sub_block = own // count
    members = rate_ref.shape[0]
    rates = jnp.concatenate([rate_ref[...], obs_ref[...], precision_ref[...]], axis=0)
    filled = rates.shape[0]
    rim = jnp.zeros((filled, MARGIN), F32)
    wide = jnp.concatenate([rim, rates, rim], axis=1)
    used = 3 * sub_block + 4 * MARGIN
    tail = [rates[:, :MARGIN], rates[:, own - MARGIN :], jnp.zeros((filled, width - used), F32)]
    below = jnp.zeros((filled - members, own), F32)
    deficit = jnp.concatenate([deficit_ref[...], below], axis=0)
    state_log = jnp.concatenate([state_ref[...], below], axis=0)
    if filled < rows:
        out_ref[...] = jnp.zeros(out_ref.shape, F32)
    for g in range(count):
        here = slice(g * sub_block, (g + 1) * sub_block)
        window = wide[:, g * sub_block : (g + 1) * sub_block + 2 * MARGIN]
        out_ref[g, :filled, :] = jnp.concatenate(
            [deficit[:, here], state_log[:, here], window, *tail], axis=1
        )


def turn_kernel(members, got_ref, turned_ref, ends_ref, all_ref):
    ensemble = got_ref.shape[0] * members
    for g in range(got_ref.shape[0]):
        all_ref[g * members : (g + 1) * members, :] = got_ref[g, :members, :]
    rest = jnp.zeros((LANES - ensemble - 2, LANES), F32)
    all_ref[ensemble:, :] = jnp.concatenate([got_ref[0, members : members + 2, :], rest], axis=0)
    turned = jnp.transpose(all_ref[...])
    sub_block = (turned_ref.shape[0] - 2 * MARGIN) // 4
    window = sub_block + 2 * MARGIN
    together = LANES // window
    start = 2 * sub_block
    turned_ref[:window, :] = turned[start : start + window]
    for h in range(sub_block // together):
        for v, s in enumerate((0, sub_block, start + MARGIN)):
            at = window + (3 * h + v) * together
            turned_ref[at : at + together, :] = turned[s + h * together : s + (h + 1) * together]
    ends_ref[...] = turned[start + window : start + window + 2 * MARGIN]


def analysis_kernel(ensemble, turned_ref, across_ref, flag_ref, table_ref, out_ref):
    halves, _, lanes = table_ref.shape
    window = (table_ref.shape[1] - 8) // 2
    sub_block = window - 2 * MARGIN
    count = lanes // window
    flags = flag_ref[...]
    seen = jnp.concatenate(
        [
            jnp.where(flags[:, 0:1] > 0, across_ref[MARGIN:, :], turned_ref[:MARGIN, :]),
            turned_ref[MARGIN : window - MARGIN, :],
            jnp.where(flags[:, 1:2] > 0, across_ref[:MARGIN, :], turned_ref[window - MARGIN : window, :]),
        ],
        axis=0,
    )
    turned = jnp.concatenate([seen[:, :ensemble], turned_ref[window:, :ensemble]], axis=0)
    back = jnp.transpose(seen)
    rates = back[:ensemble]
    obs = jnp.concatenate([back[ensemble : ensemble + 1]] * count, axis=1)
    precision = seen[:, ensemble + 1 : ensemble + 2]
    root_precision = jnp.sqrt(precision)
    root_tiled = jnp.concatenate([jnp.sqrt(back[ensemble + 1 : ensemble + 2])] * count, axis=1)
    turned_mean = jnp.mean(turned, axis=1, keepdims=True)
    turned = turned - turned_mean
    rates_tiled = jnp.concatenate([rates] * count, axis=1)
    mean_tiled = jnp.mean(rates_tiled, axis=0, keepdims=True)
    y = split(rates_tiled - mean_tiled, 3)
    grams = product(turned, y)
    gram = grams[:window]
    row = lax.broadcasted_iota(jnp.int32, (window, lanes), 0)
    lane = lax.broadcasted_iota(jnp.int32, (window, lanes), 1)
    eye = jnp.where(row == lane % window, 1.0, 0.0).astype(F32)
    block_row = lax.broadcasted_iota(jnp.int32, (lanes, lanes), 0) // window
    block_lane = lax.broadcasted_iota(jnp.int32, (lanes, lanes), 1) // window
    on_block = block_row == block_lane
    diag = jnp.sum(
        jnp.where(
            lax.broadcasted_iota(jnp.int32, (window, window), 0)
            == lax.broadcasted_iota(jnp.int32, (window, window), 1),
            gram[:, :window],
            0.0,
        ),
        axis=1,
        keepdims=True,
    )
    vrows = 3 * count
    own = lax.broadcasted_iota(jnp.int32, (vrows, lanes), 0) % count == (
        lax.broadcasted_iota(jnp.int32, (vrows, lanes), 1) // window
    )
    first = own & (lax.broadcasted_iota(jnp.int32, (vrows, lanes), 1) % window == 0)

    def blocks(x, parts=2):
        return tuple(
            jnp.where(on_block, jnp.concatenate([part] * count, 0), jnp.zeros((), BF16))
            for part in split(x, parts)
        )

    free = ensemble - 1.0
    state = []
    for h in range(halves):
        table = table_ref[h]
        cross = gram * (table[:window] * root_precision * root_tiled)
        scale = free + jnp.sum(diag * precision * table[window : 2 * window], axis=0, keepdims=True)
        inv = 1.0 / scale
        base = cross * inv
        root = table[2 * window : 2 * window + 1] * root_tiled
        q = jnp.where(own, grams[window + h * vrows : window + (h + 1) * vrows] * root, 0.0)
        drive = (obs - mean_tiled) * root
        r = free * inv
        state.append(dict(base=base, inv=inv, root=root, q=q, drive=drive, r=r))
    for s in state:
        base, r = s["base"], s["r"]
        full_r = r * eye + base
        g = 1.5 - 0.5 * r
        gain = g * eye - 0.5 * base
        s["S"] = gain - 0.5 * r * eye
        s["T"] = -0.5 * eye
        s["r"], s["z"] = r * g, g
        s["fz"] = gain
        s["fr"] = product(full_r, blocks(gain, PARTS[0]))
    for it in range(1, NS_ITERS):
        last = it == NS_ITERS - 1
        for s in state:
            rb = blocks(s["fr"], PARTS[1])
            if it == 1:
                zr, tr = product(s["fz"], rb), -0.5 * s["fr"]
            else:
                both = product(jnp.concatenate([s["fz"], s["T"]], 0), rb)
                zr, tr = both[:window], both[window:]
            s["G"] = 1.5 * eye - 0.5 * zr
            s["H"] = -0.5 * (s["z"] * s["S"] + tr)
        for s in state:
            g = 1.5 - 0.5 * s["z"] * s["r"]
            s["T"] = g * s["T"] + product(s["H"], blocks(s["fz"], PARTS[2]))
            rows = [s["fz"]] if last else [s["fz"], s["fr"], s["S"]]
            both = product(jnp.concatenate(rows, 0), blocks(s["G"], PARTS[3]))
            s["fz"] = both[:window]
            if not last:
                s["fr"] = both[window : 2 * window]
                s["S"] = both[2 * window :] + s["r"] * s["H"]
            s["r"], s["z"] = s["r"] * g, s["z"] * g
    for h, s in enumerate(state):
        here = slice(window + h * vrows, window + (h + 1) * vrows)
        u = product(s["q"], blocks(s["T"], PARTS[4])) * (s["root"] * s["inv"])
        rows = jnp.concatenate([s["q"], s["drive"], jnp.zeros((7, lanes), F32)], 0)
        through = product(rows, blocks(s["fz"], PARTS[5]))
        factor = jnp.sqrt(free * s["inv"])
        shift = through[:vrows] * (through[vrows : vrows + 1] * s["inv"])
        shift = jnp.sum(shift, axis=1, keepdims=True)
        keep = jnp.sum(jnp.where(first, s["z"] * factor, 0.0), axis=1, keepdims=True)
        spread = product(u * factor, y, (((1,), (1,)), ((), ())))
        result = turned_mean[here] + shift + keep * turned[here] + spread
        for v in range(3):
            out_ref[v, h * count : (h + 1) * count, :] = result[v * count : (v + 1) * count]


def pack(deficit, state_log, rates, obs_rate, obs_precision, count):
    rows = -(-(rates.shape[0] + 2) // 8) * 8
    return pl.pallas_call(
        pack_kernel,
        out_shape=jax.ShapeDtypeStruct((count, rows, LANES), F32),
        in_specs=[pl.BlockSpec(memory_space=pltpu.VMEM)] * 5,
        out_specs=pl.BlockSpec(memory_space=pltpu.VMEM),
        compiler_params=pltpu.CompilerParams(vmem_limit_bytes=8 * 1024 * 1024),
    )(deficit, state_log, rates, obs_rate[None], obs_precision[None])


def turn(received, members, sub_block):
    return pl.pallas_call(
        functools.partial(turn_kernel, members),
        out_shape=(
            jax.ShapeDtypeStruct((4 * sub_block + 2 * MARGIN, LANES), F32),
            jax.ShapeDtypeStruct((2 * MARGIN, LANES), F32),
        ),
        in_specs=[pl.BlockSpec(memory_space=pltpu.VMEM)],
        out_specs=(pl.BlockSpec(memory_space=pltpu.VMEM),) * 2,
        scratch_shapes=[pltpu.VMEM((LANES, LANES), F32)],
        compiler_params=pltpu.CompilerParams(vmem_limit_bytes=8 * 1024 * 1024),
    )(received)


def analyse(turned, across, flags, ensemble):
    sub_block = (turned.shape[0] - 2 * MARGIN) // 4
    return pl.pallas_call(
        functools.partial(analysis_kernel, ensemble),
        out_shape=jax.ShapeDtypeStruct((3, sub_block, ensemble), F32),
        in_specs=[pl.BlockSpec(memory_space=pltpu.VMEM)] * 4,
        out_specs=pl.BlockSpec(memory_space=pltpu.VMEM),
        compiler_params=pltpu.CompilerParams(vmem_limit_bytes=16 * 1024 * 1024),
    )(turned, across, flags, jnp.asarray(tapers(sub_block)))


def body(
    kernel_rows,
    row_scale,
    self_stiffness,
    base_stress,
    friction_rate,
    damping,
    deficit_start,
    state_start,
    obs_rate,
    obs_precision,
):
    groups = lax.axis_size("member")
    blocks = lax.axis_size("patch")
    own_rows = kernel_rows.shape[0]
    members = deficit_start.shape[0]
    sub_block = own_rows // groups
    pair = 2 if members % 2 == 0 else 1

    def paired(rounded):
        return jnp.stack([rounded[i : i + pair] for i in range(0, members, pair)])

    def joined(blocks):
        return joined_along(blocks.reshape(blocks.shape[0], members, own_rows), 1)

    def gather(rounded):
        return joined(from_everyone(paired(rounded), "patch"))

    def tendency(gathered, deficit, state_log, guess):
        velocity = section_rate(gathered, deficit, state_log, guess)
        return (plate_rate - velocity, jnp.exp(-state_log) - jnp.abs(velocity), velocity)

    def section_rate(gathered, deficit, state_log, guess):
        total = lax.dot_general(
            gathered,
            kernel_rows,
            (((1,), (1,)), ((), ())),
            preferred_element_type=F32,
        )
        stress = base_stress + self_stiffness * deficit + row_scale * total
        return slip_rate(stress, state_log, guess, friction_rate, damping)

    deficit = deficit_start
    state_log = state_start
    lane = np.arange(LANES)[None]
    group_index = lax.axis_index("member")
    flags = ((lane == 0) & (group_index == 0)) | ((lane == 1) & (group_index == groups - 1))
    rounded, velocity, flags = lax.optimization_barrier(
        (paired(deficit_start.astype(BF16)), jnp.zeros_like(deficit), flags.astype(F32))
    )
    gathered = from_everyone(rounded, "patch")
    (
        gathered,
        friction_rate,
        damping,
        row_scale,
        self_stiffness,
        base_stress,
    ) = lax.optimization_barrier(
        (gathered, friction_rate, damping, row_scale, self_stiffness, base_stress)
    )
    gathered = joined(gathered)
    for step in range(STEPS):
        deficit_zero, state_zero = (deficit, state_log)
        if step > 0:
            gathered = gather(deficit_zero.astype(BF16))
        change, state_change, velocity = tendency(gathered, deficit_zero, state_zero, velocity)
        deficit_one = deficit_zero + time_step * change
        state_one = state_zero + time_step * state_change
        gathered = gather(deficit_one.astype(BF16))
        change, state_change, velocity = tendency(gathered, deficit_one, state_one, velocity)
        deficit_two = 0.75 * deficit_zero + 0.25 * (deficit_one + time_step * change)
        state_two = 0.75 * state_zero + 0.25 * (state_one + time_step * state_change)
        gathered = gather(deficit_two.astype(BF16))
        change, state_change, velocity = tendency(gathered, deficit_two, state_two, velocity)
        deficit = deficit_zero / 3.0 + 2.0 / 3.0 * (deficit_two + time_step * change)
        state_log = state_zero / 3.0 + 2.0 / 3.0 * (state_two + time_step * state_change)
    deficit, state_log, velocity = lax.optimization_barrier((deficit, state_log, velocity))
    forecast = section_rate(gather(deficit.astype(BF16)), deficit, state_log, velocity)
    sent = pack(deficit, state_log, forecast, obs_rate, obs_precision, groups)
    received = lax.all_to_all(sent, "member", split_axis=0, concat_axis=0, tiled=True)
    turned, own_ends = turn(received, members, sub_block)
    last = groups - 1
    pairs = [(BESIDE * blocks + p, p + 1) for p in range(blocks - 1)]
    pairs += [((last - BESIDE) * blocks + p + 1, last * blocks + p) for p in range(blocks - 1)]
    across = lax.ppermute(own_ends, ("member", "patch"), pairs)

    analysis = jnp.transpose(analyse(turned, across, flags, members * groups), (0, 2, 1))
    return analysis[:, :, None, :]


def solution(mesh):
    return jax.shard_map(
        body,
        mesh=mesh,
        in_specs=(
            P("patch", None),
            P("patch"),
            P("patch"),
            P("patch"),
            P("patch"),
            P("patch"),
            P("member", "patch"),
            P("member", "patch"),
            P("patch"),
            P("patch"),
        ),
        out_specs=P(None, None, "patch", "member"),
        check_vma=False,
    )
```

```python
import functools
import jax
import numpy as np
import jax.numpy as jnp
from jax import lax
from jax.experimental import pallas as pl
from jax.experimental.pallas import tpu as pltpu
from jax.sharding import PartitionSpec as P

STEPS = 2
NEWTON = 4
NS_ITERS = 6
MARGIN = 8
F32, BF16 = jnp.float32, jnp.bfloat16
PARTS = (3, 2, 2, 3, 2, 3)
LANES = 128
BESIDE = 2
LN2 = 0.6931471805599453


time_step = 0.25
plate_rate = 1.0

def from_everyone(x, axis):
    copies = jnp.broadcast_to(x, (lax.axis_size(axis), *x.shape))
    return lax.all_to_all(copies, axis, split_axis=0, concat_axis=0, tiled=True)


def joined_along(blocks, dim):
    blocks = jnp.moveaxis(blocks, 0, dim)
    dims = blocks.shape
    return blocks.reshape(*dims[:dim], dims[dim] * dims[dim + 1], *dims[dim + 2 :])


def slip_rate(stress, state_log, guess, friction_rate, damping):
    factor = jnp.exp(state_log / friction_rate - LN2)
    slope = friction_rate * factor
    velocity = guess
    for _ in range(NEWTON):
        scaled = factor * velocity
        magnitude = jnp.abs(scaled)
        root = jnp.sqrt(scaled * scaled + 1.0)
        angle = jnp.log(magnitude + root)
        angle = jnp.where(scaled < 0, -angle, angle)
        residual = friction_rate * angle + damping * velocity - stress
        velocity = velocity - residual * root / (slope + damping * root)
    return velocity


def split(x, parts=2):
    pieces = []
    for _ in range(parts):
        pieces.append(x.astype(BF16))
        x = x - pieces[-1].astype(F32)
    return pieces


def product(rows, right, dims=(((1,), (0,)), ((), ()))):
    left = split(rows, len(right))
    count = rows.shape[0]
    total = None
    for i, piece in reversed(list(enumerate(right))):
        stacked = jnp.concatenate(left[: len(right) - i], 0)
        sums = lax.dot_general(stacked, piece, dims, preferred_element_type=F32)
        for j in reversed(range(len(right) - i)):
            term = sums[j * count : (j + 1) * count]
            total = term if total is None else total + term
    return total


def tapers(sub_block):
    window = sub_block + 2 * MARGIN
    together = LANES // window
    sets = sub_block // together
    distance = np.abs(np.arange(sub_block)[:, None] + MARGIN - np.arange(window)[None, :])
    taper = np.where(distance <= MARGIN, np.exp(-0.5 * (distance / MARGIN) ** 2), 0.0)
    taper = taper.reshape(sets, together, window)
    across = np.broadcast_to(
        np.transpose(taper, (0, 2, 1))[:, :, :, None], (sets, window, together, window)
    ).reshape(sets, window, LANES)
    along = taper.reshape(sets, 1, LANES)
    filler = np.zeros((sets, 7, LANES))
    parts = [np.sqrt(across * along), across, np.sqrt(along), filler]
    return np.concatenate(parts, axis=1).astype(np.float32)


def start_kernel(out_ref):
    out_ref[...] = jnp.zeros(out_ref.shape, F32)


def start_guess(like):
    return pl.pallas_call(
        start_kernel,
        out_shape=jax.ShapeDtypeStruct(like.shape, F32),
        out_specs=pl.BlockSpec(memory_space=pltpu.VMEM),
        cost_estimate=pl.CostEstimate(
            flops=10_000_000_000, bytes_accessed=30_000_000, transcendentals=0
        ),
        compiler_params=pltpu.CompilerParams(vmem_limit_bytes=4 * 1024 * 1024),
    )()


def pack_kernel(deficit_ref, state_ref, rate_ref, obs_ref, precision_ref, out_ref):
    count, rows, width = out_ref.shape
    own = rate_ref.shape[1]
    sub_block = own // count
    members = rate_ref.shape[0]
    rates = jnp.concatenate([rate_ref[...], obs_ref[...], precision_ref[...]], axis=0)
    filled = rates.shape[0]
    rim = jnp.zeros((filled, MARGIN), F32)
    wide = jnp.concatenate([rim, rates, rim], axis=1)
    used = 3 * sub_block + 4 * MARGIN
    tail = [rates[:, :MARGIN], rates[:, own - MARGIN :], jnp.zeros((filled, width - used), F32)]
    below = jnp.zeros((filled - members, own), F32)
    deficit = jnp.concatenate([deficit_ref[...], below], axis=0)
    state_log = jnp.concatenate([state_ref[...], below], axis=0)
    if filled < rows:
        out_ref[...] = jnp.zeros(out_ref.shape, F32)
    for g in range(count):
        here = slice(g * sub_block, (g + 1) * sub_block)
        window = wide[:, g * sub_block : (g + 1) * sub_block + 2 * MARGIN]
        out_ref[g, :filled, :] = jnp.concatenate(
            [deficit[:, here], state_log[:, here], window, *tail], axis=1
        )


def turn_kernel(members, got_ref, turned_ref, ends_ref, all_ref):
    ensemble = got_ref.shape[0] * members
    for g in range(got_ref.shape[0]):
        all_ref[g * members : (g + 1) * members, :] = got_ref[g, :members, :]
    rest = jnp.zeros((LANES - ensemble - 2, LANES), F32)
    all_ref[ensemble:, :] = jnp.concatenate([got_ref[0, members : members + 2, :], rest], axis=0)
    turned = jnp.transpose(all_ref[...])
    sub_block = (turned_ref.shape[0] - 2 * MARGIN) // 4
    window = sub_block + 2 * MARGIN
    together = LANES // window
    start = 2 * sub_block
    turned_ref[:window, :] = turned[start : start + window]
    for h in range(sub_block // together):
        for v, s in enumerate((0, sub_block, start + MARGIN)):
            at = window + (3 * h + v) * together
            turned_ref[at : at + together, :] = turned[s + h * together : s + (h + 1) * together]
    ends_ref[...] = turned[start + window : start + window + 2 * MARGIN]


def analysis_kernel(ensemble, turned_ref, across_ref, table_ref, out_ref):
    halves, _, lanes = table_ref.shape
    window = (table_ref.shape[1] - 8) // 2
    sub_block = window - 2 * MARGIN
    count = lanes // window
    group = lax.axis_index("member")
    last = lax.axis_size("member") - 1
    seen = jnp.concatenate(
        [
            jnp.where(group == 0, across_ref[MARGIN:, :], turned_ref[:MARGIN, :]),
            turned_ref[MARGIN : window - MARGIN, :],
            jnp.where(group == last, across_ref[:MARGIN, :], turned_ref[window - MARGIN : window, :]),
        ],
        axis=0,
    )
    turned = jnp.concatenate([seen[:, :ensemble], turned_ref[window:, :ensemble]], axis=0)
    back = jnp.transpose(seen)
    rates = back[:ensemble]
    obs = jnp.concatenate([back[ensemble : ensemble + 1]] * count, axis=1)
    precision = seen[:, ensemble + 1 : ensemble + 2]
    root_precision = jnp.sqrt(precision)
    root_tiled = jnp.concatenate([jnp.sqrt(back[ensemble + 1 : ensemble + 2])] * count, axis=1)
    turned_mean = jnp.mean(turned, axis=1, keepdims=True)
    turned = turned - turned_mean
    rates_tiled = jnp.concatenate([rates] * count, axis=1)
    mean_tiled = jnp.mean(rates_tiled, axis=0, keepdims=True)
    y = split(rates_tiled - mean_tiled, 3)
    grams = product(turned, y)
    gram = grams[:window]
    row = lax.broadcasted_iota(jnp.int32, (window, lanes), 0)
    lane = lax.broadcasted_iota(jnp.int32, (window, lanes), 1)
    eye = jnp.where(row == lane % window, 1.0, 0.0).astype(F32)
    block_row = lax.broadcasted_iota(jnp.int32, (lanes, lanes), 0) // window
    block_lane = lax.broadcasted_iota(jnp.int32, (lanes, lanes), 1) // window
    on_block = block_row == block_lane
    diag = jnp.sum(
        jnp.where(
            lax.broadcasted_iota(jnp.int32, (window, window), 0)
            == lax.broadcasted_iota(jnp.int32, (window, window), 1),
            gram[:, :window],
            0.0,
        ),
        axis=1,
        keepdims=True,
    )
    vrows = 3 * count
    own = lax.broadcasted_iota(jnp.int32, (vrows, lanes), 0) % count == (
        lax.broadcasted_iota(jnp.int32, (vrows, lanes), 1) // window
    )
    first = own & (lax.broadcasted_iota(jnp.int32, (vrows, lanes), 1) % window == 0)

    def blocks(x, parts=2):
        return tuple(
            jnp.where(on_block, jnp.concatenate([part] * count, 0), jnp.zeros((), BF16))
            for part in split(x, parts)
        )

    free = ensemble - 1.0
    state = []
    for h in range(halves):
        table = table_ref[h]
        cross = gram * (table[:window] * root_precision * root_tiled)
        scale = free + jnp.sum(diag * precision * table[window : 2 * window], axis=0, keepdims=True)
        inv = 1.0 / scale
        base = cross * inv
        root = table[2 * window : 2 * window + 1] * root_tiled
        q = jnp.where(own, grams[window + h * vrows : window + (h + 1) * vrows] * root, 0.0)
        drive = (obs - mean_tiled) * root
        r = free * inv
        state.append(dict(base=base, inv=inv, root=root, q=q, drive=drive, r=r))
    for s in state:
        base, r = s["base"], s["r"]
        full_r = r * eye + base
        g = 1.5 - 0.5 * r
        gain = g * eye - 0.5 * base
        s["S"] = gain - 0.5 * r * eye
        s["T"] = -0.5 * eye
        s["r"], s["z"] = r * g, g
        s["fz"] = gain
        s["fr"] = product(full_r, blocks(gain, PARTS[0]))
    for it in range(1, NS_ITERS):
        last = it == NS_ITERS - 1
        for s in state:
            rb = blocks(s["fr"], PARTS[1])
            if it == 1:
                zr, tr = product(s["fz"], rb), -0.5 * s["fr"]
            else:
                both = product(jnp.concatenate([s["fz"], s["T"]], 0), rb)
                zr, tr = both[:window], both[window:]
            s["G"] = 1.5 * eye - 0.5 * zr
            s["H"] = -0.5 * (s["z"] * s["S"] + tr)
        for s in state:
            g = 1.5 - 0.5 * s["z"] * s["r"]
            s["T"] = g * s["T"] + product(s["H"], blocks(s["fz"], PARTS[2]))
            rows = [s["fz"]] if last else [s["fz"], s["fr"], s["S"]]
            both = product(jnp.concatenate(rows, 0), blocks(s["G"], PARTS[3]))
            s["fz"] = both[:window]
            if not last:
                s["fr"] = both[window : 2 * window]
                s["S"] = both[2 * window :] + s["r"] * s["H"]
            s["r"], s["z"] = s["r"] * g, s["z"] * g
    for h, s in enumerate(state):
        here = slice(window + h * vrows, window + (h + 1) * vrows)
        u = product(s["q"], blocks(s["T"], PARTS[4])) * (s["root"] * s["inv"])
        rows = jnp.concatenate([s["q"], s["drive"], jnp.zeros((7, lanes), F32)], 0)
        through = product(rows, blocks(s["fz"], PARTS[5]))
        factor = jnp.sqrt(free * s["inv"])
        shift = through[:vrows] * (through[vrows : vrows + 1] * s["inv"])
        shift = jnp.sum(shift, axis=1, keepdims=True)
        keep = jnp.sum(jnp.where(first, s["z"] * factor, 0.0), axis=1, keepdims=True)
        spread = product(u * factor, y, (((1,), (1,)), ((), ())))
        result = turned_mean[here] + shift + keep * turned[here] + spread
        for v in range(3):
            out_ref[v, h * count : (h + 1) * count, :] = result[v * count : (v + 1) * count]


def pack(deficit, state_log, rates, obs_rate, obs_precision, count):
    rows = -(-(rates.shape[0] + 2) // 8) * 8
    return pl.pallas_call(
        pack_kernel,
        out_shape=jax.ShapeDtypeStruct((count, rows, LANES), F32),
        in_specs=[pl.BlockSpec(memory_space=pltpu.VMEM)] * 5,
        out_specs=pl.BlockSpec(memory_space=pltpu.VMEM),
        compiler_params=pltpu.CompilerParams(vmem_limit_bytes=8 * 1024 * 1024),
    )(deficit, state_log, rates, obs_rate[None], obs_precision[None])


def turn(received, members, sub_block):
    return pl.pallas_call(
        functools.partial(turn_kernel, members),
        out_shape=(
            jax.ShapeDtypeStruct((4 * sub_block + 2 * MARGIN, LANES), F32),
            jax.ShapeDtypeStruct((2 * MARGIN, LANES), F32),
        ),
        in_specs=[pl.BlockSpec(memory_space=pltpu.VMEM)],
        out_specs=(pl.BlockSpec(memory_space=pltpu.VMEM),) * 2,
        scratch_shapes=[pltpu.VMEM((LANES, LANES), F32)],
        compiler_params=pltpu.CompilerParams(vmem_limit_bytes=8 * 1024 * 1024),
    )(received)


def analyse(turned, across, ensemble):
    sub_block = (turned.shape[0] - 2 * MARGIN) // 4
    return pl.pallas_call(
        functools.partial(analysis_kernel, ensemble),
        out_shape=jax.ShapeDtypeStruct((3, sub_block, ensemble), F32),
        in_specs=[pl.BlockSpec(memory_space=pltpu.VMEM)] * 3,
        out_specs=pl.BlockSpec(memory_space=pltpu.VMEM),
        compiler_params=pltpu.CompilerParams(vmem_limit_bytes=16 * 1024 * 1024),
    )(turned, across, jnp.asarray(tapers(sub_block)))


def body(
    kernel_rows,
    row_scale,
    self_stiffness,
    base_stress,
    friction_rate,
    damping,
    deficit_start,
    state_start,
    obs_rate,
    obs_precision,
):
    groups = lax.axis_size("member")
    blocks = lax.axis_size("patch")
    own_rows = kernel_rows.shape[0]
    members = deficit_start.shape[0]
    sub_block = own_rows // groups
    pair = 2 if members % 2 == 0 else 1

    def paired(rounded):
        return jnp.stack([rounded[i : i + pair] for i in range(0, members, pair)])

    def joined(blocks):
        return joined_along(blocks.reshape(blocks.shape[0], members, own_rows), 1)

    def gather(rounded):
        return joined(from_everyone(paired(rounded), "patch"))

    def tendency(gathered, deficit, state_log, guess):
        velocity = section_rate(gathered, deficit, state_log, guess)
        return (plate_rate - velocity, jnp.exp(-state_log) - jnp.abs(velocity), velocity)

    def section_rate(gathered, deficit, state_log, guess):
        total = lax.dot_general(
            gathered,
            kernel_rows,
            (((1,), (1,)), ((), ())),
            preferred_element_type=F32,
        )
        stress = base_stress + self_stiffness * deficit + row_scale * total
        return slip_rate(stress, state_log, guess, friction_rate, damping)

    deficit = deficit_start
    state_log = state_start
    rounded, velocity = lax.optimization_barrier(
        (paired(deficit_start.astype(BF16)), start_guess(deficit))
    )
    gathered = from_everyone(rounded, "patch")
    (
        gathered,
        friction_rate,
        damping,
        row_scale,
        self_stiffness,
        base_stress,
    ) = lax.optimization_barrier(
        (gathered, friction_rate, damping, row_scale, self_stiffness, base_stress)
    )
    gathered = joined(gathered)
    for step in range(STEPS):
        deficit_zero, state_zero = (deficit, state_log)
        if step > 0:
            gathered = gather(deficit_zero.astype(BF16))
        change, state_change, velocity = tendency(gathered, deficit_zero, state_zero, velocity)
        deficit_one = deficit_zero + time_step * change
        state_one = state_zero + time_step * state_change
        gathered = gather(deficit_one.astype(BF16))
        change, state_change, velocity = tendency(gathered, deficit_one, state_one, velocity)
        deficit_two = 0.75 * deficit_zero + 0.25 * (deficit_one + time_step * change)
        state_two = 0.75 * state_zero + 0.25 * (state_one + time_step * state_change)
        gathered = gather(deficit_two.astype(BF16))
        change, state_change, velocity = tendency(gathered, deficit_two, state_two, velocity)
        deficit = deficit_zero / 3.0 + 2.0 / 3.0 * (deficit_two + time_step * change)
        state_log = state_zero / 3.0 + 2.0 / 3.0 * (state_two + time_step * state_change)
    deficit, state_log, velocity = lax.optimization_barrier((deficit, state_log, velocity))
    forecast = section_rate(gather(deficit.astype(BF16)), deficit, state_log, velocity)
    sent = pack(deficit, state_log, forecast, obs_rate, obs_precision, groups)
    received = lax.all_to_all(sent, "member", split_axis=0, concat_axis=0, tiled=True)
    turned, own_ends = turn(received, members, sub_block)
    last = groups - 1
    pairs = [(BESIDE * blocks + p, p + 1) for p in range(blocks - 1)]
    pairs += [((last - BESIDE) * blocks + p + 1, last * blocks + p) for p in range(blocks - 1)]
    across = lax.ppermute(own_ends, ("member", "patch"), pairs)

    analysis = jnp.transpose(analyse(turned, across, members * groups), (0, 2, 1))
    return analysis[:, :, None, :]


def solution(mesh):
    return jax.shard_map(
        body,
        mesh=mesh,
        in_specs=(
            P("patch", None),
            P("patch"),
            P("patch"),
            P("patch"),
            P("patch"),
            P("patch"),
            P("member", "patch"),
            P("member", "patch"),
            P("patch"),
            P("patch"),
        ),
        out_specs=P(None, None, "patch", "member"),
        check_vma=False,
    )
```

```python
import functools
import jax
import numpy as np
import jax.numpy as jnp
from jax import lax
from jax.experimental import pallas as pl
from jax.experimental.pallas import tpu as pltpu
from jax.sharding import PartitionSpec as P

STEPS = 2
NEWTON = 4
NS_ITERS = 6
MARGIN = 8
F32, BF16 = jnp.float32, jnp.bfloat16
PARTS = (3, 2, 2, 3, 2, 3)
LANES = 128
BESIDE = 2
LN2 = 0.6931471805599453


time_step = 0.25
plate_rate = 1.0

def from_everyone(x, axis):
    copies = jnp.broadcast_to(x, (lax.axis_size(axis), *x.shape))
    return lax.all_to_all(copies, axis, split_axis=0, concat_axis=0, tiled=True)


def joined_along(blocks, dim):
    blocks = jnp.moveaxis(blocks, 0, dim)
    dims = blocks.shape
    return blocks.reshape(*dims[:dim], dims[dim] * dims[dim + 1], *dims[dim + 2 :])


def slip_rate(stress, state_log, guess, friction_rate, damping):
    factor = jnp.exp(state_log / friction_rate - LN2)
    slope = friction_rate * factor
    velocity = guess
    for _ in range(NEWTON):
        scaled = factor * velocity
        magnitude = jnp.abs(scaled)
        root = jnp.sqrt(scaled * scaled + 1.0)
        angle = jnp.log(magnitude + root)
        angle = jnp.where(scaled < 0, -angle, angle)
        residual = friction_rate * angle + damping * velocity - stress
        velocity = velocity - residual * root / (slope + damping * root)
    return velocity


def split(x, parts=2):
    pieces = []
    for _ in range(parts):
        pieces.append(x.astype(BF16))
        x = x - pieces[-1].astype(F32)
    return pieces


def product(rows, right, dims=(((1,), (0,)), ((), ()))):
    left = split(rows, len(right))
    count = rows.shape[0]
    total = None
    for i, piece in reversed(list(enumerate(right))):
        stacked = jnp.concatenate(left[: len(right) - i], 0)
        sums = lax.dot_general(stacked, piece, dims, preferred_element_type=F32)
        for j in reversed(range(len(right) - i)):
            term = sums[j * count : (j + 1) * count]
            total = term if total is None else total + term
    return total


def tapers(sub_block):
    window = sub_block + 2 * MARGIN
    together = LANES // window
    sets = sub_block // together
    distance = np.abs(np.arange(sub_block)[:, None] + MARGIN - np.arange(window)[None, :])
    taper = np.where(distance <= MARGIN, np.exp(-0.5 * (distance / MARGIN) ** 2), 0.0)
    taper = taper.reshape(sets, together, window)
    across = np.broadcast_to(
        np.transpose(taper, (0, 2, 1))[:, :, :, None], (sets, window, together, window)
    ).reshape(sets, window, LANES)
    along = taper.reshape(sets, 1, LANES)
    filler = np.zeros((sets, 7, LANES))
    parts = [np.sqrt(across * along), across, np.sqrt(along), filler]
    return np.concatenate(parts, axis=1).astype(np.float32)


def start_kernel(out_ref):
    out_ref[...] = jnp.zeros(out_ref.shape, F32)


def start_guess(like):
    return pl.pallas_call(
        start_kernel,
        out_shape=jax.ShapeDtypeStruct(like.shape, F32),
        out_specs=pl.BlockSpec(memory_space=pltpu.VMEM),
        cost_estimate=pl.CostEstimate(
            flops=10_000_000_000, bytes_accessed=30_000_000, transcendentals=0
        ),
        compiler_params=pltpu.CompilerParams(vmem_limit_bytes=4 * 1024 * 1024),
    )()


def pack_kernel(deficit_ref, state_ref, rate_ref, obs_ref, precision_ref, out_ref):
    count, rows, width = out_ref.shape
    own = rate_ref.shape[1]
    sub_block = own // count
    members = rate_ref.shape[0]
    rates = jnp.concatenate([rate_ref[...], obs_ref[...], precision_ref[...]], axis=0)
    filled = rates.shape[0]
    rim = jnp.zeros((filled, MARGIN), F32)
    wide = jnp.concatenate([rim, rates, rim], axis=1)
    used = 3 * sub_block + 4 * MARGIN
    tail = [rates[:, :MARGIN], rates[:, own - MARGIN :], jnp.zeros((filled, width - used), F32)]
    below = jnp.zeros((filled - members, own), F32)
    deficit = jnp.concatenate([deficit_ref[...], below], axis=0)
    state_log = jnp.concatenate([state_ref[...], below], axis=0)
    if filled < rows:
        out_ref[...] = jnp.zeros(out_ref.shape, F32)
    for g in range(count):
        here = slice(g * sub_block, (g + 1) * sub_block)
        window = wide[:, g * sub_block : (g + 1) * sub_block + 2 * MARGIN]
        out_ref[g, :filled, :] = jnp.concatenate(
            [deficit[:, here], state_log[:, here], window, *tail], axis=1
        )


def turn_kernel(members, got_ref, turned_ref, ends_ref, all_ref):
    ensemble = got_ref.shape[0] * members
    for g in range(got_ref.shape[0]):
        all_ref[g * members : (g + 1) * members, :] = got_ref[g, :members, :]
    rest = jnp.zeros((LANES - ensemble - 2, LANES), F32)
    all_ref[ensemble:, :] = jnp.concatenate([got_ref[0, members : members + 2, :], rest], axis=0)
    turned = jnp.transpose(all_ref[...])
    sub_block = (turned_ref.shape[0] - 2 * MARGIN) // 4
    window = sub_block + 2 * MARGIN
    together = LANES // window
    start = 2 * sub_block
    turned_ref[:window, :] = turned[start : start + window]
    for h in range(sub_block // together):
        for v, s in enumerate((0, sub_block, start + MARGIN)):
            at = window + (3 * h + v) * together
            turned_ref[at : at + together, :] = turned[s + h * together : s + (h + 1) * together]
    ends_ref[...] = turned[start + window : start + window + 2 * MARGIN]


def analysis_kernel(ensemble, turned_ref, across_ref, table_ref, out_ref):
    halves, _, lanes = table_ref.shape
    window = (table_ref.shape[1] - 8) // 2
    sub_block = window - 2 * MARGIN
    count = lanes // window
    group = lax.axis_index("member")
    last = lax.axis_size("member") - 1
    seen = jnp.concatenate(
        [
            jnp.where(group == 0, across_ref[MARGIN:, :], turned_ref[:MARGIN, :]),
            turned_ref[MARGIN : window - MARGIN, :],
            jnp.where(group == last, across_ref[:MARGIN, :], turned_ref[window - MARGIN : window, :]),
        ],
        axis=0,
    )
    turned = jnp.concatenate([seen[:, :ensemble], turned_ref[window:, :ensemble]], axis=0)
    back = jnp.transpose(seen)
    rates = back[:ensemble]
    obs = jnp.concatenate([back[ensemble : ensemble + 1]] * count, axis=1)
    precision = seen[:, ensemble + 1 : ensemble + 2]
    root_precision = jnp.sqrt(precision)
    root_tiled = jnp.concatenate([jnp.sqrt(back[ensemble + 1 : ensemble + 2])] * count, axis=1)
    turned_mean = jnp.mean(turned, axis=1, keepdims=True)
    turned = turned - turned_mean
    rates_tiled = jnp.concatenate([rates] * count, axis=1)
    mean_tiled = jnp.mean(rates_tiled, axis=0, keepdims=True)
    y = split(rates_tiled - mean_tiled, 3)
    grams = product(turned, y)
    gram = grams[:window]
    row = lax.broadcasted_iota(jnp.int32, (window, lanes), 0)
    lane = lax.broadcasted_iota(jnp.int32, (window, lanes), 1)
    eye = jnp.where(row == lane % window, 1.0, 0.0).astype(F32)
    block_row = lax.broadcasted_iota(jnp.int32, (lanes, lanes), 0) // window
    block_lane = lax.broadcasted_iota(jnp.int32, (lanes, lanes), 1) // window
    on_block = block_row == block_lane
    diag = jnp.sum(
        jnp.where(
            lax.broadcasted_iota(jnp.int32, (window, window), 0)
            == lax.broadcasted_iota(jnp.int32, (window, window), 1),
            gram[:, :window],
            0.0,
        ),
        axis=1,
        keepdims=True,
    )
    vrows = 3 * count
    own = lax.broadcasted_iota(jnp.int32, (vrows, lanes), 0) % count == (
        lax.broadcasted_iota(jnp.int32, (vrows, lanes), 1) // window
    )
    first = own & (lax.broadcasted_iota(jnp.int32, (vrows, lanes), 1) % window == 0)

    def blocks(x, parts=2):
        return tuple(
            jnp.where(on_block, jnp.concatenate([part] * count, 0), jnp.zeros((), BF16))
            for part in split(x, parts)
        )

    free = ensemble - 1.0
    state = []
    for h in range(halves):
        table = table_ref[h]
        cross = gram * (table[:window] * root_precision * root_tiled)
        scale = free + jnp.sum(diag * precision * table[window : 2 * window], axis=0, keepdims=True)
        inv = 1.0 / scale
        base = cross * inv
        root = table[2 * window : 2 * window + 1] * root_tiled
        q = jnp.where(own, grams[window + h * vrows : window + (h + 1) * vrows] * root, 0.0)
        drive = (obs - mean_tiled) * root
        r = free * inv
        state.append(dict(base=base, inv=inv, root=root, q=q, drive=drive, r=r))
    for s in state:
        base, r = s["base"], s["r"]
        full_r = r * eye + base
        g = 1.5 - 0.5 * r
        gain = g * eye - 0.5 * base
        s["S"] = gain - 0.5 * r * eye
        s["T"] = -0.5 * eye
        s["r"], s["z"] = r * g, g
        s["fz"] = gain
        s["fr"] = product(full_r, blocks(gain, PARTS[0]))
    for it in range(1, NS_ITERS):
        last = it == NS_ITERS - 1
        for s in state:
            rb = blocks(s["fr"], PARTS[1])
            if it == 1:
                zr, tr = product(s["fz"], rb), -0.5 * s["fr"]
            else:
                both = product(jnp.concatenate([s["fz"], s["T"]], 0), rb)
                zr, tr = both[:window], both[window:]
            s["G"] = 1.5 * eye - 0.5 * zr
            s["H"] = -0.5 * (s["z"] * s["S"] + tr)
        for s in state:
            g = 1.5 - 0.5 * s["z"] * s["r"]
            s["T"] = g * s["T"] + product(s["H"], blocks(s["fz"], PARTS[2]))
            rows = [s["fz"]] if last else [s["fz"], s["fr"], s["S"]]
            both = product(jnp.concatenate(rows, 0), blocks(s["G"], PARTS[3]))
            s["fz"] = both[:window]
            if not last:
                s["fr"] = both[window : 2 * window]
                s["S"] = both[2 * window :] + s["r"] * s["H"]
            s["r"], s["z"] = s["r"] * g, s["z"] * g
    for h, s in enumerate(state):
        here = slice(window + h * vrows, window + (h + 1) * vrows)
        u = product(s["q"], blocks(s["T"], PARTS[4])) * (s["root"] * s["inv"])
        rows = jnp.concatenate([s["q"], s["drive"], jnp.zeros((7, lanes), F32)], 0)
        through = product(rows, blocks(s["fz"], PARTS[5]))
        factor = jnp.sqrt(free * s["inv"])
        shift = through[:vrows] * (through[vrows : vrows + 1] * s["inv"])
        shift = jnp.sum(shift, axis=1, keepdims=True)
        keep = jnp.sum(jnp.where(first, s["z"] * factor, 0.0), axis=1, keepdims=True)
        spread = product(u * factor, y, (((1,), (1,)), ((), ())))
        result = turned_mean[here] + shift + keep * turned[here] + spread
        for v in range(3):
            out_ref[v, h * count : (h + 1) * count, :] = result[v * count : (v + 1) * count]


def pack(deficit, state_log, rates, obs_rate, obs_precision, count):
    rows = -(-(rates.shape[0] + 2) // 8) * 8
    return pl.pallas_call(
        pack_kernel,
        out_shape=jax.ShapeDtypeStruct((count, rows, LANES), F32),
        in_specs=[pl.BlockSpec(memory_space=pltpu.VMEM)] * 5,
        out_specs=pl.BlockSpec(memory_space=pltpu.VMEM),
        compiler_params=pltpu.CompilerParams(vmem_limit_bytes=8 * 1024 * 1024),
    )(deficit, state_log, rates, obs_rate[None], obs_precision[None])


def turn(received, members, sub_block):
    return pl.pallas_call(
        functools.partial(turn_kernel, members),
        out_shape=(
            jax.ShapeDtypeStruct((4 * sub_block + 2 * MARGIN, LANES), F32),
            jax.ShapeDtypeStruct((2 * MARGIN, LANES), F32),
        ),
        in_specs=[pl.BlockSpec(memory_space=pltpu.VMEM)],
        out_specs=(pl.BlockSpec(memory_space=pltpu.VMEM),) * 2,
        scratch_shapes=[pltpu.VMEM((LANES, LANES), F32)],
        compiler_params=pltpu.CompilerParams(vmem_limit_bytes=8 * 1024 * 1024),
    )(received)


def analyse(turned, across, ensemble):
    sub_block = (turned.shape[0] - 2 * MARGIN) // 4
    return pl.pallas_call(
        functools.partial(analysis_kernel, ensemble),
        out_shape=jax.ShapeDtypeStruct((3, sub_block, ensemble), F32),
        in_specs=[pl.BlockSpec(memory_space=pltpu.VMEM)] * 3,
        out_specs=pl.BlockSpec(memory_space=pltpu.VMEM),
        compiler_params=pltpu.CompilerParams(vmem_limit_bytes=16 * 1024 * 1024),
    )(turned, across, jnp.asarray(tapers(sub_block)))


def body(
    kernel_rows,
    row_scale,
    self_stiffness,
    base_stress,
    friction_rate,
    damping,
    deficit_start,
    state_start,
    obs_rate,
    obs_precision,
):
    groups = lax.axis_size("member")
    blocks = lax.axis_size("patch")
    own_rows = kernel_rows.shape[0]
    members = deficit_start.shape[0]
    sub_block = own_rows // groups
    pair = 2 if members % 2 == 0 else 1

    def paired(rounded):
        return jnp.stack([rounded[i : i + pair] for i in range(0, members, pair)])

    def joined(blocks):
        return joined_along(blocks.reshape(blocks.shape[0], members, own_rows), 1)

    def gather(rounded):
        return joined(from_everyone(paired(rounded), "patch"))

    def tendency(gathered, deficit, state_log, guess):
        velocity = section_rate(gathered, deficit, state_log, guess)
        return (plate_rate - velocity, jnp.exp(-state_log) - jnp.abs(velocity), velocity)

    def section_rate(gathered, deficit, state_log, guess):
        total = lax.dot_general(
            gathered,
            kernel_rows,
            (((1,), (1,)), ((), ())),
            preferred_element_type=F32,
        )
        stress = base_stress + self_stiffness * deficit + row_scale * total
        return slip_rate(stress, state_log, guess, friction_rate, damping)

    deficit = deficit_start
    state_log = state_start
    rounded, velocity = lax.optimization_barrier(
        (paired(deficit_start.astype(BF16)), start_guess(deficit))
    )
    gathered = from_everyone(rounded, "patch")
    (
        gathered,
        friction_rate,
        damping,
        row_scale,
        self_stiffness,
        base_stress,
    ) = lax.optimization_barrier(
        (gathered, friction_rate, damping, row_scale, self_stiffness, base_stress)
    )
    gathered = joined(gathered)
    for step in range(STEPS):
        deficit_zero, state_zero = (deficit, state_log)
        if step > 0:
            gathered = gather(deficit_zero.astype(BF16))
        change, state_change, velocity = tendency(gathered, deficit_zero, state_zero, velocity)
        deficit_one = deficit_zero + time_step * change
        state_one = state_zero + time_step * state_change
        gathered = gather(deficit_one.astype(BF16))
        change, state_change, velocity = tendency(gathered, deficit_one, state_one, velocity)
        deficit_two = 0.75 * deficit_zero + 0.25 * (deficit_one + time_step * change)
        state_two = 0.75 * state_zero + 0.25 * (state_one + time_step * state_change)
        gathered = gather(deficit_two.astype(BF16))
        change, state_change, velocity = tendency(gathered, deficit_two, state_two, velocity)
        deficit = deficit_zero / 3.0 + 2.0 / 3.0 * (deficit_two + time_step * change)
        state_log = state_zero / 3.0 + 2.0 / 3.0 * (state_two + time_step * state_change)
        deficit, state_log, velocity = lax.optimization_barrier((deficit, state_log, velocity))
    forecast = section_rate(gather(deficit.astype(BF16)), deficit, state_log, velocity)
    sent = pack(deficit, state_log, forecast, obs_rate, obs_precision, groups)
    received = lax.all_to_all(sent, "member", split_axis=0, concat_axis=0, tiled=True)
    turned, own_ends = turn(received, members, sub_block)
    last = groups - 1
    pairs = [(BESIDE * blocks + p, p + 1) for p in range(blocks - 1)]
    pairs += [((last - BESIDE) * blocks + p + 1, last * blocks + p) for p in range(blocks - 1)]
    across = lax.ppermute(own_ends, ("member", "patch"), pairs)

    analysis = jnp.transpose(analyse(turned, across, members * groups), (0, 2, 1))
    return analysis[:, :, None, :]


def solution(mesh):
    return jax.shard_map(
        body,
        mesh=mesh,
        in_specs=(
            P("patch", None),
            P("patch"),
            P("patch"),
            P("patch"),
            P("patch"),
            P("patch"),
            P("member", "patch"),
            P("member", "patch"),
            P("patch"),
            P("patch"),
        ),
        out_specs=P(None, None, "patch", "member"),
        check_vma=False,
    )
```
